256 devices in a mesh: section: 2 (over y_hi), tensor: 8 (over y_lo, x), feat: 16 (over z, core).
Axes of the slice: x: 4, y: 4 (y_hi: 2, y_lo: 2; y = y_hi * 2 + y_lo), z: 8, core: 2. Of those that a mesh axis runs over, the one named last changes fastest.
Arguments:
- new_queries: bfloat16 [512, 16384], P(('section', 'feat'), 'tensor'), may hold values from -6 to 6
- new_keys: bfloat16 [512, 1024], P(('section', 'feat'), 'tensor'), may hold values from -6 to 6
- new_values: bfloat16 [512, 1024], P(('section', 'feat'), 'tensor'), may hold values from -6 to 6
- key_cache: bfloat16 [512, 256, 1024], P(('section', 'feat'), None, 'tensor'), may hold values from -6 to 6
- value_cache: bfloat16 [512, 256, 1024], P(('section', 'feat'), None, 'tensor'), may hold values from -6 to 6
- cache_lengths: int32 [512], P(('section', 'feat')), may hold values from 2 to 256
- residual: bfloat16 [512, 16384], P('section', 'feat'), may hold values from -48 to 48
- output_weight: bfloat16 [16384, 16384], P('tensor', 'feat'), may hold values from -0.75 to 0.75
- encoder_weight: bfloat16 [16384, 16384], P('feat', ('section', 'tensor')), may hold values from -0.046875 to 0.046875
- encoder_bias: float32 [16384], P(('section', 'tensor')), may hold values from -3 to 3
- decoder_weight: bfloat16 [16384, 16384], P(('section', 'tensor'), 'feat'), may hold values from -0.046875 to 0.046875
- decoder_bias: float32 [16384], P('feat'), may hold values from -3 to 3
- clamp_ids: int32 [512, 8], replicated, may hold values from 0 to 16383
- clamp_values: int32 [512, 8], replicated, may hold values from 0 to 47
Outputs:
- steered: bfloat16 [512, 16384], P(('section', 'tensor'), 'feat')
- latents: bfloat16 [512, 16384], P(None, ('section', 'tensor'))
The draws below stay inside these ranges and needn't reach their ends.
All inputs are finite; a program needn't handle non-finite values.
Results may differ from the reference program's by a relative error of at most 0.0061.
Values may be sent and summed in bfloat16 or wider, within the bound.
A program may use at most 64 MiB of HBM per device.

```python
import math
import jax
import jax.numpy as jnp
from jax import lax

D = 16384
HEADS = 128
KV = 8
HD = 128
LAT = 16384
CLAMPS = 8
CTX = 256
ROWS = 512


def draw_new_queries(key, part):
    key = jax.random.fold_in(key, 7)
    sampled = jnp.clip(jax.random.normal(key, (ROWS, HEADS * HD), jnp.float32), -6.0, 6.0)
    return sampled.astype(jnp.bfloat16)


def draw_key_cache(key, part):
    key = jax.random.fold_in(key, 9)
    sampled = jnp.clip(jax.random.normal(key, (ROWS, CTX, KV * HD), jnp.float32), -6.0, 6.0)
    return sampled.astype(jnp.bfloat16)


def draw_residual(key, part):
    key = jax.random.fold_in(key, 5)
    sampled = jnp.clip(jax.random.normal(key, (ROWS, D), jnp.float32), -6.0, 6.0)
    position = jnp.arange(D).astype(jnp.float32) / D
    rising = 0.6 * jnp.power(3.0, position)
    sampled = sampled * rising[None, :]
    return sampled.astype(jnp.bfloat16)


def touch_ends(entries, stream_key, low, largest):
    longest = entries.shape.index(max(entries.shape))
    spots = []
    for shift in (0, 1):
        where = [jax.random.randint(jax.random.fold_in(stream_key, axis), (), 0, length) for axis, length in enumerate(entries.shape)]
        where[longest] = (where[longest] + shift) % entries.shape[longest]
        spots.append(tuple(where))
    return entries.at[spots[0]].set(low).at[spots[1]].set(largest)


def levels(rng, extent, shards, smallest, largest):
    level, own = 1.0, jax.random.fold_in(rng, 6)
    for axis_at, blocks in shards:
        heights = jnp.exp(jax.random.uniform(jax.random.fold_in(own, axis_at), (blocks,), jnp.float32, smallest / len(shards), largest / len(shards)))
        level = level * jnp.repeat(heights, extent[axis_at] // blocks).reshape([-1 if axis == axis_at else 1 for axis in range(len(extent))])
    return level


def noise(rng, extent, width, most, pieces=(), dtype=jnp.bfloat16):
    entries = jax.random.normal(rng, extent, jnp.float32) * width
    if len(pieces) > 0:
        entries = levels(rng, extent, pieces, -0.22, 0.18) * entries
    return jnp.clip(entries, min=-most, max=most).astype(dtype)


def setup_inputs(seed: int = 0) -> dict:
    streams_of = jax.random.split(jax.random.key(seed), 15)
    new_queries = draw_new_queries(jax.random.fold_in(streams_of[14], 71), 0)
    new_keys = noise(streams_of[1], (ROWS, KV * HD), 1.0, 6.0, ((0, 32), (1, 8)))
    new_values = noise(streams_of[2], (ROWS, KV * HD), 1.0, 6.0, ((0, 32), (1, 8)))
    key_cache = draw_key_cache(jax.random.fold_in(streams_of[14], 71), 0)
    value_cache = noise(streams_of[4], (ROWS, CTX, KV * HD), 1.0, 6.0, ((0, 32), (2, 8)))
    cache_lengths = touch_ends(jax.random.randint(streams_of[5], (ROWS,), 2, CTX + 1), jax.random.fold_in(streams_of[5], 1), 2, CTX).astype(jnp.int32)
    residual = draw_residual(jax.random.fold_in(streams_of[14], 71), 0)
    output_weight = noise(streams_of[7], (HEADS * HD, D), (HEADS * HD // CTX) ** -0.5, 0.75, ((0, 8), (1, 16)))
    encoder_weight = noise(streams_of[8], (D, LAT), D ** -0.5, 0.046875, ((0, 16), (1, 16)))
    encoder_bias = noise(streams_of[9], (LAT,), 0.5, 3.0, ((0, 16),), jnp.float32)
    decoder_weight = noise(streams_of[10], (LAT, D), LAT ** -0.5, 0.046875, ((0, 16), (1, 16)))
    decoder_bias = noise(streams_of[11], (D,), 0.3, 3.0, ((0, 16),), jnp.float32)
    clamp_ids = touch_ends(jax.random.randint(streams_of[12], (ROWS, CLAMPS), 0, LAT), jax.random.fold_in(streams_of[12], 1), 0, LAT - 1).astype(jnp.int32)
    clamp_values = touch_ends(jax.random.randint(streams_of[13], (ROWS, CLAMPS), 0, 48), jax.random.fold_in(streams_of[13], 1), 0, 47).astype(jnp.int32)
    return {"new_queries": new_queries, "new_keys": new_keys, "new_values": new_values, "key_cache": key_cache, "value_cache": value_cache, "cache_lengths": cache_lengths, "residual": residual, "output_weight": output_weight, "encoder_weight": encoder_weight, "encoder_bias": encoder_bias, "decoder_weight": decoder_weight, "decoder_bias": decoder_bias, "clamp_ids": clamp_ids, "clamp_values": clamp_values}


NEGATIVE = -1e+30
EPSILON = 1e-05

def reference(new_queries, new_keys, new_values, key_cache, value_cache, cache_lengths, residual, output_weight, encoder_weight, encoder_bias, decoder_weight, decoder_bias, clamp_ids, clamp_values):
    group_size = HEADS // KV
    score_scale = 1.0 / math.sqrt(HD)
    visible = (jnp.arange(CTX)[None, :] < cache_lengths[:, None])[:, None, :]
    outputs = []
    for head_group in range(KV):
        lane_start = head_group * HD
        cached_keys = key_cache[:, :, lane_start:lane_start + HD].astype(jnp.float32)
        cached_values = value_cache[:, :, lane_start:lane_start + HD].astype(jnp.float32)
        fresh_keys = new_keys[:, lane_start:lane_start + HD].astype(jnp.float32)
        fresh_values = new_values[:, lane_start:lane_start + HD].astype(jnp.float32)
        query_start = head_group * group_size * HD
        queries = new_queries[:, query_start:query_start + group_size * HD].reshape(ROWS, group_size, HD).astype(jnp.float32)
        scores = jnp.einsum('rgd,rpd->rgp', queries, cached_keys, precision=lax.Precision.HIGHEST) * score_scale
        scores = jnp.where(visible, scores, NEGATIVE)
        own_score = jnp.einsum('rgd,rd->rg', queries, fresh_keys, precision=lax.Precision.HIGHEST) * score_scale
        highest = jnp.maximum(lax.optimization_barrier(jnp.max(scores, -1)), own_score)
        weights_raw = jnp.where(visible, jnp.exp(scores - highest[..., None]), 0.0)
        own_raw = jnp.exp(own_score - highest)
        totals = lax.optimization_barrier(jnp.sum(weights_raw, -1)) + own_raw
        weights = lax.optimization_barrier(weights_raw.astype(jnp.bfloat16)).astype(jnp.float32)
        own_weight = lax.optimization_barrier(own_raw.astype(jnp.bfloat16)).astype(jnp.float32)
        blended = jnp.einsum('rgp,rpd->rgd', weights, cached_values, precision=lax.Precision.HIGHEST)
        blended = blended + own_weight[..., None] * fresh_values[:, None, :]
        outputs.append((blended / totals[..., None]).reshape(ROWS, group_size * HD))
    attended = jnp.concatenate(outputs, 1).astype(jnp.bfloat16)
    hidden = (residual.astype(jnp.float32) + jnp.dot(attended, output_weight, preferred_element_type=jnp.float32)).astype(jnp.bfloat16)
    hidden_wide = hidden.astype(jnp.float32)
    scale_rows = jnp.sqrt(lax.optimization_barrier(jnp.mean(jnp.square(hidden_wide), -1)) + EPSILON)
    centered = (hidden_wide / scale_rows[:, None] - decoder_bias).astype(jnp.bfloat16)
    encoded = jnp.dot(centered, encoder_weight, preferred_element_type=jnp.float32)
    latents = jnp.maximum(encoded + encoder_bias, 0.0).astype(jnp.bfloat16)
    columns = jnp.arange(LAT)
    chosen = jnp.full((ROWS, LAT), -1.0, jnp.float32)
    for clamp_slot in range(CLAMPS):
        matches = clamp_ids[:, clamp_slot:clamp_slot + 1] == columns[None, :]
        target = clamp_values[:, clamp_slot:clamp_slot + 1].astype(jnp.float32)
        chosen = jnp.where(matches, jnp.maximum(chosen, target), chosen)
    clamped = jnp.where(chosen >= 0.0, chosen, latents.astype(jnp.float32)).astype(jnp.bfloat16)
    picked = jnp.take_along_axis(clamped.astype(jnp.float32), clamp_ids, 1) - jnp.take_along_axis(latents.astype(jnp.float32), clamp_ids, 1)
    same_id = clamp_ids[:, :, None] == clamp_ids[:, None, :]
    earlier = jnp.arange(CLAMPS)[None, :] < jnp.arange(CLAMPS)[:, None]
    repeated = jnp.any(same_id & earlier[None, :, :], -1)
    differences = jnp.where(repeated, 0.0, picked)
    decoder_rows = decoder_weight[clamp_ids].astype(jnp.float32)
    change = jnp.einsum('rk,rkd->rd', differences, decoder_rows, precision=lax.Precision.HIGHEST)
    steered = (hidden_wide + scale_rows[:, None] * change).astype(jnp.bfloat16)
    return (steered, latents)
```

```python
import functools
import math

import jax
import jax.numpy as jnp
from jax import lax
from jax.experimental import pallas as pl
from jax.experimental.pallas import tpu as pltpu
from jax.sharding import PartitionSpec as P

D = 16384
HD = 128
EPSILON = 1e-05
NEGATIVE = -1e30
MESH = pl.DeviceIdType.MESH
F32 = jnp.float32
BF16 = jnp.bfloat16

TILE = 256


def kernel(
    q_hbm, nk_ref, nv_ref, kc_hbm, vc_hbm, lens_ref, res_hbm, wo_hbm, we_hbm,
    be_ref, wd_hbm, bd_ref, ids_ref, vals_ref,
    steered_hbm, latents_hbm,
    q_in, kc, vc, res, wo, we, wd, q_heads, o_heads,
    ids_col, vals_col, chosen, target_out,
    att, proj, proj_send, proj_recv, hid, info, scales,
    enc, enc_send, pair_recv, z_send, enc_recv, lat, chg_send, chg_recv, out_rows,
    in_sem, out_sem,
    b_s, b_r, bp_s, bp_r, c_s, c_r, d_s, d_r, i_s, i_r, s_s, s_r,
    ep_s, ep_r, e_s, e_r, l_s, l_r, lp_s, lp_r, f_s, f_r,
):
    me_f = lax.axis_index("feat")
    me_t = lax.axis_index("tensor")
    me_a = lax.axis_index("section") * 8 + me_t
    z = me_f // 2
    core = lax.rem(me_f, 2)
    partner = me_f + 1 - 2 * core

    def feat_id(f):
        return {"feat": f}

    def plane_id(a):
        return {"section": a // 8, "tensor": lax.rem(a, 8)}

    def push(src, dst, ss, rs, device):
        return pltpu.make_async_remote_copy(
            src_ref=src, dst_ref=dst, send_sem=ss, recv_sem=rs,
            device_id=device, device_id_type=MESH,
        )

    barrier = pltpu.get_barrier_semaphore()

    def announce(k, carry):
        pl.semaphore_signal(barrier, inc=1, device_id=feat_id(lax.rem(me_f + k, 16)), device_id_type=MESH)
        pl.semaphore_signal(barrier, inc=1, device_id=plane_id(lax.rem(me_a + k, 16)), device_id_type=MESH)
        return carry

    lax.fori_loop(1, 16, announce, 0)

    loads = [
        pltpu.make_async_copy(q_hbm, q_in, in_sem.at[0]),
        pltpu.make_async_copy(kc_hbm, kc, in_sem.at[1]),
        pltpu.make_async_copy(vc_hbm, vc, in_sem.at[2]),
        pltpu.make_async_copy(wo_hbm, wo, in_sem.at[3]),
        pltpu.make_async_copy(we_hbm, we, in_sem.at[4]),
        pltpu.make_async_copy(wd_hbm, wd, in_sem.at[5]),
        pltpu.make_async_copy(res_hbm.at[pl.ds(me_t * 32, 32)], res, in_sem.at[6]),
    ]
    for load in loads:
        load.start()

    loads[0].wait()
    for h in range(16):
        q_heads[:, h, :] = q_in[:, h * HD : (h + 1) * HD].astype(F32)
    fresh_keys = nk_ref[...].astype(F32)
    fresh_values = nv_ref[...].astype(F32)
    loads[1].wait()
    loads[2].wait()
    score_scale = 1.0 / math.sqrt(HD)
    position = lax.broadcasted_iota(jnp.int32, (16, 256), 1)
    for r in range(16):
        queries = q_heads[r]
        scores = lax.dot_general(
            queries.astype(BF16), kc[r], (((1,), (1,)), ((), ())), preferred_element_type=F32
        ) * score_scale
        scores = jnp.where(position < lens_ref[r], scores, NEGATIVE)
        own_score = jnp.sum(queries * fresh_keys[r : r + 1], -1, keepdims=True) * score_scale
        highest = jnp.maximum(jnp.max(scores, -1, keepdims=True), own_score)
        raw = jnp.exp(scores - highest)
        own_raw = jnp.exp(own_score - highest)
        totals = jnp.sum(raw, -1, keepdims=True) + own_raw
        blended = jnp.dot(raw.astype(BF16), vc[r], preferred_element_type=F32)
        blended = blended + own_raw.astype(BF16).astype(F32) * fresh_values[r : r + 1]
        o_heads[r] = blended / totals
    for h in range(16):
        att[me_f, :, h * HD : (h + 1) * HD] = o_heads[:, h, :].astype(BF16)

    pl.semaphore_wait(barrier, 30)

    def gather_z(buf, zs, zr, ps, pr):
        def out(k):
            return push(buf.at[me_f], buf.at[me_f], zs.at[k], zr.at[k], feat_id(lax.rem(me_f + 2 * k, 16)))

        def across(k):
            src = lax.rem(me_f + 16 - 2 * k, 16)
            return push(buf.at[src], buf.at[src], ps.at[k], pr.at[k], feat_id(partner))

        def start():
            def body(k, carry):
                out(k).start()
                return carry

            lax.fori_loop(1, 8, body, 0)
            across(0).start()

        def forward():
            def body(k, carry):
                out(k).wait_recv()
                across(k).start()
                return carry

            lax.fori_loop(1, 8, body, 0)

        def finish():
            def body(k, carry):
                across(k).wait_recv()
                return carry

            lax.fori_loop(0, 8, body, 0)

        def drain():
            def body(k, carry):
                out(k).wait_send()
                across(k).wait_send()
                return carry

            lax.fori_loop(1, 8, body, 0)
            across(0).wait_send()

        return start, forward, finish, drain

    b_start, b_forward, b_finish, b_drain = gather_z(att, b_s, b_r, bp_s, bp_r)
    b_start()

    ids_col[...] = ids_ref[...].astype(F32).T
    vals_col[...] = vals_ref[...].astype(F32).T
    first_latent = (me_a * 1024).astype(F32)

    def choose(i, carry):
        rows = pl.ds(pl.multiple_of(i * 32, 32), 32)
        ids = ids_col[rows, :] - first_latent
        values = vals_col[rows, :]
        column = lax.broadcasted_iota(jnp.int32, (32, 1024), 1).astype(F32)
        best = jnp.full((32, 1024), -1.0, F32)
        for j in range(8):
            best = jnp.where(ids[:, j : j + 1] == column, jnp.maximum(best, values[:, j : j + 1]), best)
        chosen[rows, :] = best.astype(BF16)
        return carry

    lax.fori_loop(0, 16, choose, 0)

    b_forward()
    loads[3].wait()
    b_finish()

    def project(n, carry):
        cols = pl.ds(pl.multiple_of(n * TILE, TILE), TILE)
        term = jnp.dot(att[...].reshape(256, 2048), wo[:, cols], preferred_element_type=F32)
        proj[:, cols] = term
        proj_send[:, cols] = term.astype(BF16)
        return carry

    lax.fori_loop(0, 1024 // TILE, project, 0)

    def c_push(k):
        peer = lax.rem(me_t + k, 8)
        rows = pl.ds(pl.multiple_of(peer * 32, 32), 32)
        return push(proj_send.at[rows], proj_recv.at[k], c_s.at[k], c_r.at[k], {"tensor": peer})

    def c_start(k, carry):
        c_push(k).start()
        return carry

    lax.fori_loop(1, 8, c_start, 0)

    loads[4].wait()
    bias = bd_ref[...]
    high = bias.astype(BF16)
    rest = bias - high.astype(F32)
    middle = rest.astype(BF16)
    low = (rest - middle.astype(F32)).astype(BF16)
    index = lax.broadcasted_iota(jnp.int32, (16, 1024), 0)
    stacked = jnp.where(
        index == 0, high.astype(F32), jnp.where(index == 1, middle.astype(F32), jnp.where(index == 2, low.astype(F32), 0.0))
    ).astype(BF16)
    for n in range(4):
        part = jnp.dot(stacked, we[:, n * 256 : (n + 1) * 256], preferred_element_type=F32)
        part = jnp.sum(part[0:8], 0, keepdims=True)
        info[me_f, 32 + 2 * n : 33 + 2 * n, :] = part[:, :128]
        info[me_f, 33 + 2 * n : 34 + 2 * n, :] = part[:, 128:]

    loads[6].wait()

    def c_sum(k, total):
        c_push(k).wait_recv()
        return total + proj_recv[k].astype(F32)

    own_rows = pl.ds(pl.multiple_of(me_t * 32, 32), 32)
    summed = lax.fori_loop(1, 8, c_sum, proj[own_rows, :])
    hid[me_a] = (res[...].astype(F32) + summed).astype(BF16)

    def d_push(k):
        return push(hid.at[me_a], hid.at[me_a], d_s.at[k], d_r.at[k], plane_id(lax.rem(me_a + k, 16)))

    def d_start(k, carry):
        d_push(k).start()
        return carry

    lax.fori_loop(1, 16, d_start, 0)

    wide = hid[me_a].astype(F32)
    squares = wide * wide
    partial = squares[:, 0:128]
    for j in range(1, 8):
        partial = partial + squares[:, j * 128 : (j + 1) * 128]
    info[me_f, 0:32, :] = partial

    def i_push(k):
        return push(info.at[me_f], info.at[me_f], i_s.at[k], i_r.at[k], feat_id(lax.rem(me_f + k, 16)))

    def i_start(k, carry):
        i_push(k).start()
        return carry

    lax.fori_loop(1, 16, i_start, 0)

    loads[5].wait()

    def target_term(n, carry):
        cols = pl.ds(pl.multiple_of(n * TILE, TILE), TILE)
        target_out[:, cols] = jnp.dot(jnp.maximum(chosen[...], 0), wd[:, cols], preferred_element_type=F32)
        return carry

    lax.fori_loop(0, 1024 // TILE, target_term, 0)

    def i_wait(k, carry):
        i_push(k).wait_recv()
        return carry

    lax.fori_loop(1, 16, i_wait, 0)
    total_info = info[0]
    for f in range(1, 16):
        total_info = total_info + info[f]
    mean = jnp.sum(total_info[0:32], -1, keepdims=True) / D
    scales[me_a] = jnp.broadcast_to(jnp.sqrt(mean + EPSILON), (32, 128))
    bias_term = total_info[32:40]

    def s_push(k):
        return push(scales.at[me_a], scales.at[me_a], s_s.at[k], s_r.at[k], plane_id(lax.rem(me_a + k, 16)))

    def s_start(k, carry):
        s_push(k).start()
        return carry

    lax.fori_loop(1, 16, s_start, 0)

    def d_wait(k, carry):
        d_push(k).wait_recv()
        return carry

    lax.fori_loop(1, 16, d_wait, 0)

    def ep_push(n):
        cols = pl.ds(pl.multiple_of(n * TILE, TILE), TILE)
        return push(
            enc_send.at[:, 1 - core, :, cols], pair_recv.at[:, :, cols], ep_s.at[n], ep_r.at[n], feat_id(partner)
        )

    def encode(n, carry):
        cols = pl.ds(pl.multiple_of(n * TILE, TILE), TILE)
        term = jnp.dot(hid[...].reshape(512, 1024), we[:, cols], preferred_element_type=F32)
        term = term.reshape(8, 2, 32, TILE)
        enc[:, :, :, cols] = term
        enc_send[:, :, :, cols] = term.astype(BF16)
        ep_push(n).start()
        return carry

    lax.fori_loop(0, 1024 // TILE, encode, 0)

    def ep_wait(n, carry):
        ep_push(n).wait_recv()
        return carry

    lax.fori_loop(0, 1024 // TILE, ep_wait, 0)

    def e_push(k):
        peer = lax.rem(z + k, 8)
        return push(z_send.at[k], enc_recv.at[k], e_s.at[k], e_r.at[k], feat_id(peer * 2 + core))

    def e_start(k, carry):
        peer = lax.rem(z + k, 8)
        z_send[k] = (enc[peer, core] + pair_recv[peer].astype(F32)).astype(BF16)
        e_push(k).start()
        return carry

    lax.fori_loop(1, 8, e_start, 0)

    def s_wait(k, carry):
        s_push(k).wait_recv()
        return carry

    lax.fori_loop(1, 16, s_wait, 0)

    def e_sum(k, total):
        e_push(k).wait_recv()
        return total + enc_recv[k].astype(F32)

    encoded = lax.fori_loop(1, 8, e_sum, enc[z, core] + pair_recv[z].astype(F32))
    inverse = 1.0 / scales[me_f]
    for j in range(8):
        cols = slice(j * 128, (j + 1) * 128)
        shift = be_ref[:, cols] - bias_term[j : j + 1]
        lat[me_f, :, cols] = jnp.maximum(encoded[:, cols] * inverse + shift, 0.0).astype(BF16)

    l_start, l_forward, l_finish, l_drain = gather_z(lat, l_s, l_r, lp_s, lp_r)
    l_start()
    l_forward()
    l_finish()
    latents_out = pltpu.make_async_copy(lat, latents_hbm, out_sem.at[0])
    latents_out.start()

    def decode(n, carry):
        cols = pl.ds(pl.multiple_of(n * TILE, TILE), TILE)
        picked = jnp.where(chosen[...] >= 0, lat[...].reshape(512, 1024), 0)
        term = target_out[:, cols] - jnp.dot(picked, wd[:, cols], preferred_element_type=F32)
        target_out[:, cols] = term
        chg_send[:, :, cols] = term.astype(BF16).reshape(16, 32, TILE)
        return carry

    lax.fori_loop(0, 1024 // TILE, decode, 0)

    def f_push(k):
        peer = lax.rem(me_a + k, 16)
        return push(chg_send.at[peer], chg_recv.at[k], f_s.at[k], f_r.at[k], plane_id(peer))

    def f_start(k, carry):
        f_push(k).start()
        return carry

    lax.fori_loop(1, 16, f_start, 0)

    def f_sum(k, total):
        f_push(k).wait_recv()
        return total + chg_recv[k].astype(F32)

    own_change = target_out[pl.ds(pl.multiple_of(me_a * 32, 32), 32), :]
    change = lax.fori_loop(1, 16, f_sum, own_change)
    own_scale = scales[me_a]
    for j in range(8):
        cols = slice(j * 128, (j + 1) * 128)
        out_rows[:, cols] = (hid[me_a, :, cols].astype(F32) + own_scale * change[:, cols]).astype(BF16)
    steered_out = pltpu.make_async_copy(out_rows, steered_hbm, out_sem.at[1])
    steered_out.start()

    b_drain()
    l_drain()

    def drain_8(k, carry):
        c_push(k).wait_send()
        e_push(k).wait_send()
        return carry

    lax.fori_loop(1, 8, drain_8, 0)

    def drain_16(k, carry):
        d_push(k).wait_send()
        i_push(k).wait_send()
        s_push(k).wait_send()
        f_push(k).wait_send()
        return carry

    lax.fori_loop(1, 16, drain_16, 0)

    def drain_tiles(n, carry):
        ep_push(n).wait_send()
        return carry

    lax.fori_loop(0, 1024 // TILE, drain_tiles, 0)
    latents_out.wait()
    steered_out.wait()


def local(
    new_queries, new_keys, new_values, key_cache, value_cache, cache_lengths, residual,
    output_weight, encoder_weight, encoder_bias, decoder_weight, decoder_bias, clamp_ids, clamp_values,
):
    hbm = pl.BlockSpec(memory_space=pl.ANY)
    vmem = pl.BlockSpec(memory_space=pltpu.VMEM)
    smem = pl.BlockSpec(memory_space=pltpu.SMEM)
    V = pltpu.VMEM
    dma = pltpu.SemaphoreType.DMA
    steered, latents = pl.pallas_call(
        kernel,
        out_shape=(
            jax.ShapeDtypeStruct((32, 1024), BF16),
            jax.ShapeDtypeStruct((16, 32, 1024), BF16),
        ),
        in_specs=[hbm, vmem, vmem, hbm, hbm, smem, hbm, hbm, hbm, vmem, hbm, vmem, vmem, vmem],
        out_specs=(hbm, hbm),
        scratch_shapes=[
            V((16, 2048), BF16), V((16, 256, 128), BF16), V((16, 256, 128), BF16), V((32, 1024), BF16),
            V((2048, 1024), BF16), V((1024, 1024), BF16), V((1024, 1024), BF16),
            V((16, 16, 128), F32), V((16, 16, 128), F32),
            V((512, 8), F32), V((512, 8), F32), V((512, 1024), BF16), V((512, 1024), F32),
            V((16, 16, 2048), BF16), V((256, 1024), F32), V((256, 1024), BF16), V((8, 32, 1024), BF16),
            V((16, 32, 1024), BF16), V((16, 40, 128), F32), V((16, 32, 128), F32),
            V((8, 2, 32, 1024), F32), V((8, 2, 32, 1024), BF16), V((8, 32, 1024), BF16),
            V((8, 32, 1024), BF16), V((8, 32, 1024), BF16), V((16, 32, 1024), BF16),
            V((16, 32, 1024), BF16), V((16, 32, 1024), BF16), V((32, 1024), BF16),
            dma((7,)), dma((2,)),
            dma((8,)), dma((8,)), dma((8,)), dma((8,)), dma((8,)), dma((8,)),
            dma((16,)), dma((16,)), dma((16,)), dma((16,)), dma((16,)), dma((16,)),
            dma((4,)), dma((4,)), dma((8,)), dma((8,)),
            dma((8,)), dma((8,)), dma((8,)), dma((8,)), dma((16,)), dma((16,)),
        ],
        compiler_params=pltpu.CompilerParams(
            collective_id=0, has_side_effects=True, vmem_limit_bytes=48 * 2**20
        ),
    )(
        new_queries, new_keys, new_values, key_cache, value_cache, cache_lengths, residual,
        output_weight, encoder_weight, encoder_bias.reshape(1, 1024), decoder_weight,
        decoder_bias.reshape(1, 1024), clamp_ids.T, clamp_values.T,
    )
    return steered, latents.reshape(512, 1024)


def solution(mesh):
    in_specs = (
        P(("section", "feat"), "tensor"),
        P(("section", "feat"), "tensor"),
        P(("section", "feat"), "tensor"),
        P(("section", "feat"), None, "tensor"),
        P(("section", "feat"), None, "tensor"),
        P(("section", "feat")),
        P("section", "feat"),
        P("tensor", "feat"),
        P("feat", ("section", "tensor")),
        P(("section", "tensor")),
        P(("section", "tensor"), "feat"),
        P("feat"),
        P(),
        P(),
    )
    out_specs = (P(("section", "tensor"), "feat"), P(None, ("section", "tensor")))
    return jax.shard_map(local, mesh=mesh, in_specs=in_specs, out_specs=out_specs, check_vma=False)
```

```python
import functools
import math

import jax
import jax.numpy as jnp
from jax import lax
from jax.experimental import pallas as pl
from jax.experimental.pallas import tpu as pltpu
from jax.sharding import PartitionSpec as P

D = 16384
HD = 128
EPSILON = 1e-05
NEGATIVE = -1e30
MESH = pl.DeviceIdType.MESH
F32 = jnp.float32
BF16 = jnp.bfloat16

TILE = 256


def kernel(
    q_hbm, nk_hbm, nv_hbm, kc_hbm, vc_hbm, lens_hbm, res_hbm, wo_hbm, we_hbm,
    be_hbm, wd_hbm, bd_hbm, ids_hbm, vals_hbm,
    steered_hbm, latents_hbm,
    q_in, kc, vc, res, wo, we, wd, nk_ref, nv_ref, lens_ref, be_ref, bd_ref, ids_ref, vals_ref, q_heads, o_heads,
    ids_col, vals_col, chosen, change, picked, current,
    att, proj, proj_send, proj_recv, hid, info, scales,
    enc, enc_send, pair_recv, z_send, enc_recv, lat, chg_send, chg_recv, out_rows,
    in_sem, out_sem,
    b_s, b_r, bp_s, bp_r, c_s, c_r, d_s, d_r, i_s, i_r, s_s, s_r,
    ep_s, ep_r, e_s, e_r, u_s, u_r, l_s, l_r, lp_s, lp_r, f_s, f_r,
):
    me_f = lax.axis_index("feat")
    me_t = lax.axis_index("tensor")
    me_a = lax.axis_index("section") * 8 + me_t
    z = me_f // 2
    core = lax.rem(me_f, 2)
    partner = me_f + 1 - 2 * core

    def feat_id(f):
        return {"feat": f}

    def plane_id(a):
        return {"section": a // 8, "tensor": lax.rem(a, 8)}

    def each(first, last, do):
        def body(k, carry):
            do(k)
            return carry

        lax.fori_loop(first, last, body, 0)

    def push(src, dst, ss, rs, device):
        return pltpu.make_async_remote_copy(
            src_ref=src, dst_ref=dst, send_sem=ss, recv_sem=rs,
            device_id=device, device_id_type=MESH,
        )

    barrier = pltpu.get_barrier_semaphore()

    def announce(k):
        pl.semaphore_signal(barrier, inc=1, device_id=feat_id(lax.rem(me_f + k, 16)), device_id_type=MESH)
        pl.semaphore_signal(barrier, inc=1, device_id=plane_id(lax.rem(me_a + k, 16)), device_id_type=MESH)

    each(1, 16, announce)

    loads = [
        pltpu.make_async_copy(q_hbm, q_in, in_sem.at[0]),
        pltpu.make_async_copy(kc_hbm, kc, in_sem.at[1]),
        pltpu.make_async_copy(vc_hbm, vc, in_sem.at[2]),
        pltpu.make_async_copy(wo_hbm, wo, in_sem.at[3]),
        pltpu.make_async_copy(we_hbm, we, in_sem.at[4]),
        pltpu.make_async_copy(wd_hbm, wd, in_sem.at[5]),
        pltpu.make_async_copy(res_hbm.at[pl.ds(me_t * 32, 32)], res, in_sem.at[6]),
        pltpu.make_async_copy(nk_hbm, nk_ref, in_sem.at[7]),
        pltpu.make_async_copy(nv_hbm, nv_ref, in_sem.at[8]),
        pltpu.make_async_copy(lens_hbm, lens_ref, in_sem.at[9]),
        pltpu.make_async_copy(ids_hbm, ids_ref, in_sem.at[10]),
        pltpu.make_async_copy(vals_hbm, vals_ref, in_sem.at[11]),
        pltpu.make_async_copy(be_hbm, be_ref, in_sem.at[12]),
        pltpu.make_async_copy(bd_hbm, bd_ref, in_sem.at[13]),
    ]
    for i in (0, 7, 8, 9, 1, 2, 3, 10, 11, 6, 12, 13, 4, 5):
        loads[i].start()

    waited = set()

    def loaded(i):
        if i not in waited:
            waited.add(i)
            loads[i].wait()

    drains = []

    loaded(0)
    for h in range(16):
        q_heads[:, h, :] = q_in[:, h * HD : (h + 1) * HD].astype(F32)
    loaded(7)
    loaded(8)
    loaded(9)
    fresh_keys = nk_ref[...].astype(F32)
    fresh_values = nv_ref[...].astype(F32)
    loaded(1)
    loaded(2)
    score_scale = 1.0 / math.sqrt(HD)
    position = lax.broadcasted_iota(jnp.int32, (16, 256), 1)
    for r in range(16):
        queries = q_heads[r]
        scores = lax.dot_general(
            queries.astype(BF16), kc[r], (((1,), (1,)), ((), ())), preferred_element_type=F32
        ) * score_scale
        scores = jnp.where(position < lens_ref[r], scores, NEGATIVE)
        own_score = jnp.sum(queries * fresh_keys[r : r + 1], -1, keepdims=True) * score_scale
        highest = jnp.maximum(jnp.max(scores, -1, keepdims=True), own_score)
        raw = jnp.exp(scores - highest)
        own_raw = jnp.exp(own_score - highest)
        totals = jnp.sum(raw, -1, keepdims=True) + own_raw
        blended = jnp.dot(raw.astype(BF16), vc[r], preferred_element_type=F32)
        blended = blended + own_raw.astype(BF16).astype(F32) * fresh_values[r : r + 1]
        o_heads[r] = blended / totals
    for h in range(16):
        att[z, core, :, h * HD : (h + 1) * HD] = o_heads[:, h, :].astype(BF16)

    pl.semaphore_wait(barrier, 30)

    def b_out(k):
        return push(att.at[z, core], att.at[z, core], b_s.at[k], b_r.at[k], feat_id(lax.rem(me_f + 2 * k, 16)))

    def b_in(k):
        piece = att.at[lax.rem(z + 8 - k, 8), core]
        return push(piece, piece, b_s.at[k], b_r.at[k], feat_id(partner))

    def b_across(k, side):
        piece = att.at[lax.rem(z + 8 - k, 8), side]
        return push(piece, piece, bp_s.at[k], bp_r.at[k], feat_id(partner))

    each(1, 8, lambda k: b_out(k).start())
    b_across(0, core).start()

    loaded(10)
    loaded(11)
    ids_col[...] = ids_ref[...].astype(F32).T
    vals_col[...] = vals_ref[...].astype(F32).T
    first_latent = (me_a * 1024).astype(F32)

    def choose(i, carry):
        rows = pl.ds(pl.multiple_of(i * 32, 32), 32)
        ids = ids_col[rows, :] - first_latent
        values = vals_col[rows, :]
        column = lax.broadcasted_iota(jnp.int32, (32, 1024), 1).astype(F32)
        best = jnp.full((32, 1024), -1.0, F32)
        for j in range(8):
            best = jnp.where(ids[:, j : j + 1] == column, jnp.maximum(best, values[:, j : j + 1]), best)
        chosen[0, i] = best[0:16].astype(BF16)
        chosen[1, i] = best[16:32].astype(BF16)
        return carry

    lax.fori_loop(0, 16, choose, 0)

    def b_relay(k):
        b_in(k).wait_recv()
        b_across(k, core).start()

    for k in (1, 7, 2, 6, 3, 5, 4):
        b_relay(k)
    loaded(3)
    each(0, 8, lambda k: b_across(k, 1 - core).wait_recv())

    def b_drain():
        each(1, 8, lambda k: b_out(k).wait_send())
        each(0, 8, lambda k: b_across(k, core).wait_send())

    drains.append(b_drain)

    def tiles(do):
        for n in range(1024 // TILE):
            do(slice(n * TILE, (n + 1) * TILE))

    def c_push(c, k):
        peer = lax.rem(me_t + k, 8)
        return push(proj_send.at[c, peer], proj_recv.at[c, k], c_s.at[c, k], c_r.at[c, k], {"tensor": peer})

    def project(c):
        def tile(cols):
            term = jnp.dot(att[:, c].reshape(128, 2048), wo[:, cols], preferred_element_type=F32).reshape(8, 16, TILE)
            proj[c, :, :, cols] = term
            proj_send[c, :, :, cols] = term.astype(BF16)

        tiles(tile)
        each(1, 8, lambda k: c_push(c, k).start())
        drains.append(lambda: each(1, 8, lambda k: c_push(c, k).wait_send()))

    project(0)
    project(1)

    loaded(4)
    loaded(13)
    bias = bd_ref[...]
    high = bias.astype(BF16)
    rest = bias - high.astype(F32)
    middle = rest.astype(BF16)
    low = (rest - middle.astype(F32)).astype(BF16)
    index = lax.broadcasted_iota(jnp.int32, (16, 1024), 0)
    stacked = jnp.where(
        index == 0, high.astype(F32), jnp.where(index == 1, middle.astype(F32), jnp.where(index == 2, low.astype(F32), 0.0))
    ).astype(BF16)
    for n in range(4):
        term = jnp.dot(stacked, we[:, n * 256 : (n + 1) * 256], preferred_element_type=F32)
        term = jnp.sum(term[0:8], 0, keepdims=True)
        info[me_f, 2 * n : 2 * n + 1, :] = term[:, :128]
        info[me_f, 2 * n + 1 : 2 * n + 2, :] = term[:, 128:]

    loaded(6)

    def d_push(c, k):
        piece = hid.at[c, me_a]
        return push(piece, piece, d_s.at[c, k], d_r.at[c, k], plane_id(lax.rem(me_a + k, 16)))

    diagonal = lax.broadcasted_iota(jnp.int32, (32, 128), 0) == lax.broadcasted_iota(jnp.int32, (32, 128), 1)

    def hidden(c):
        total = proj[c, me_t] + res[c * 16 : (c + 1) * 16].astype(F32)
        for k in range(1, 8):
            c_push(c, k).wait_recv()
            total = total + proj_recv[c, k].astype(F32)
        total = total.astype(BF16)
        hid[c, me_a] = total
        each(1, 16, lambda k: d_push(c, k).start())
        drains.append(lambda: each(1, 16, lambda k: d_push(c, k).wait_send()))
        wide = total.astype(F32)
        squares = wide * wide
        partial = squares[:, 0:128]
        for j in range(1, 8):
            partial = partial + squares[:, j * 128 : (j + 1) * 128]
        return jnp.sum(partial, -1, keepdims=True)

    sums = [hidden(0), hidden(1)]
    row = sum(jnp.sum(jnp.where(diagonal[16 * c : 16 * c + 16], sums[c], 0.0), 0, keepdims=True) for c in (0, 1))
    info[me_f, 8:16, :] = jnp.broadcast_to(row, (8, 128))

    def i_push(k):
        return push(info.at[me_f], info.at[me_f], i_s.at[k], i_r.at[k], feat_id(lax.rem(me_f + k, 16)))

    each(1, 16, lambda k: i_push(k).start())
    drains.append(lambda: each(1, 16, lambda k: i_push(k).wait_send()))

    loaded(5)

    def target_tile(c, cols):
        term = jnp.dot(jnp.maximum(chosen[c].reshape(256, 1024), 0), wd[:, cols], preferred_element_type=F32)
        change[c, :, :, cols] = term.reshape(16, 16, TILE)

    tiles(lambda cols: target_tile(0, cols))
    tiles(lambda cols: target_tile(1, cols))

    def ep_push(c, n):
        cols = slice(n * 512, (n + 1) * 512)
        return push(
            enc_send.at[c, :, 1 - core, :, cols], pair_recv.at[c, :, :, cols],
            ep_s.at[c, n], ep_r.at[c, n], feat_id(partner),
        )

    def encode(c):
        each(1, 16, lambda k: d_push(c, k).wait_recv())

        def tile(cols):
            term = jnp.dot(hid[c].reshape(256, 1024), we[:, cols], preferred_element_type=F32)
            term = term.reshape(8, 2, 16, TILE)
            enc[c, :, :, :, cols] = term
            enc_send[c, :, :, :, cols] = term.astype(BF16)
            if cols.stop % 512 == 0:
                ep_push(c, cols.stop // 512 - 1).start()

        tiles(tile)
        drains.append(lambda: [ep_push(c, n).wait_send() for n in (0, 1)])

    def e_push(c, k):
        peer = lax.rem(z + k, 8)
        return push(z_send.at[c, k], enc_recv.at[c, k], e_s.at[c, k], e_r.at[c, k], feat_id(peer * 2 + core))

    def exchange(c):
        for n in (0, 1):
            ep_push(c, n).wait_recv()

        def one(k):
            peer = lax.rem(z + k, 8)
            z_send[c, k] = (enc[c, peer, core] + pair_recv[c, peer].astype(F32)).astype(BF16)
            e_push(c, k).start()

        for k in (4, 3, 5, 2, 6, 1, 7):
            one(k)
        drains.append(lambda: each(1, 8, lambda k: e_push(c, k).wait_send()))

    encode(0)
    exchange(0)

    each(1, 16, lambda k: i_push(k).wait_recv())
    total_info = info[0]
    for f in range(1, 16):
        total_info = total_info + info[f]
    scales[me_a] = jnp.sqrt(total_info[8:16] / D + EPSILON)
    bias_term = total_info[0:8]

    def s_push(k):
        return push(scales.at[me_a], scales.at[me_a], s_s.at[k], s_r.at[k], plane_id(lax.rem(me_a + k, 16)))

    each(1, 16, lambda k: s_push(k).start())
    drains.append(lambda: each(1, 16, lambda k: s_push(k).wait_send()))

    def as_column(a):
        row = jnp.broadcast_to(scales[a, 0:1], (32, 128))
        return jnp.sum(jnp.where(diagonal, row, 0.0), -1, keepdims=True)

    encode(1)
    exchange(1)

    each(1, 16, lambda k: s_push(k).wait_recv())
    loaded(12)
    inverse = 1.0 / as_column(me_f)
    lane = lax.broadcasted_iota(jnp.int32, (16, 128), 1)
    column = lax.broadcasted_iota(jnp.int32, (16, 1024), 1).astype(F32)

    def row_ids(c, f):
        return ids_col[pl.ds(pl.multiple_of(f * 32 + c * 16, 16), 16), :] - first_latent

    def u_push(c, k):
        piece = current.at[c, me_f]
        return push(piece, piece, u_s.at[c, k], u_r.at[c, k], feat_id(lax.rem(me_f + k, 16)))

    def latents(c):
        total = enc[c, z, core] + pair_recv[c, z].astype(F32)
        for k in (1, 7, 2, 6, 3, 5, 4):
            e_push(c, k).wait_recv()
            total = total + enc_recv[c, k].astype(F32)
        scale = inverse[c * 16 : (c + 1) * 16]
        for j in range(8):
            cols = slice(j * 128, (j + 1) * 128)
            shift = be_ref[:, cols] - bias_term[j : j + 1]
            lat[c, z, core, :, cols] = jnp.maximum(total[:, cols] * scale + shift, 0.0).astype(BF16)
        mine = lat[c, z, core].astype(F32)
        ids = row_ids(c, me_f)
        held = jnp.zeros((16, 128), F32)
        for j in range(8):
            value = jnp.sum(jnp.where(ids[:, j : j + 1] == column, mine, 0.0), -1, keepdims=True)
            held = jnp.where(lane == j, value, held)
        current[c, me_f] = held.astype(BF16)
        each(1, 16, lambda k: u_push(c, k).start())
        drains.append(lambda: each(1, 16, lambda k: u_push(c, k).wait_send()))

    latents(0)
    latents(1)

    def l_out(c, k):
        piece = lat.at[c, z, core]
        return push(piece, piece, l_s.at[c, k], l_r.at[c, k], feat_id(lax.rem(me_f + 2 * k, 16)))

    def l_in(c, k):
        piece = lat.at[c, lax.rem(z + 8 - k, 8), core]
        return push(piece, piece, l_s.at[c, k], l_r.at[c, k], feat_id(partner))

    def l_across(c, k, side):
        piece = lat.at[c, lax.rem(z + 8 - k, 8), side]
        return push(piece, piece, lp_s.at[c, k], lp_r.at[c, k], feat_id(partner))

    for c in (0, 1):
        each(1, 8, lambda k: l_out(c, k).start())
        l_across(c, 0, core).start()

    def f_push(c, k):
        peer = lax.rem(me_a + k, 16)
        return push(chg_send.at[c, peer], chg_recv.at[c, k], f_s.at[c, k], f_r.at[c, k], plane_id(peer))

    def decode(c):
        each(1, 16, lambda k: u_push(c, k).wait_recv())

        def rebuild(f):
            ids = row_ids(c, f)
            values = current[c, f].astype(F32)
            best = jnp.zeros((16, 1024), F32)
            for j in range(8):
                best = jnp.where(ids[:, j : j + 1] == column, values[:, j : j + 1], best)
            picked[f] = best.astype(BF16)

        each(0, 16, rebuild)

        def tile(cols):
            term = jnp.dot(picked[...].reshape(256, 1024), wd[:, cols], preferred_element_type=F32)
            term = change[c, :, :, cols] - term.reshape(16, 16, TILE)
            change[c, :, :, cols] = term
            chg_send[c, :, :, cols] = term.astype(BF16)

        tiles(tile)
        each(1, 16, lambda k: f_push(c, k).start())
        drains.append(lambda: each(1, 16, lambda k: f_push(c, k).wait_send()))

    decode(0)
    decode(1)

    for c in (0, 1):
        for k in (1, 7, 2, 6, 3, 5, 4):
            l_in(c, k).wait_recv()
            l_across(c, k, core).start()

    own_scale = as_column(me_a)
    for c in (0, 1):
        total = change[c, me_a]
        for k in range(1, 16):
            f_push(c, k).wait_recv()
            total = total + chg_recv[c, k].astype(F32)
        rows = slice(c * 16, (c + 1) * 16)
        out_rows[rows] = (hid[c, me_a].astype(F32) + own_scale[rows] * total).astype(BF16)
    steered_out = pltpu.make_async_copy(out_rows, steered_hbm, out_sem.at[2])
    steered_out.start()

    latents_out = []
    for c in (0, 1):
        each(0, 8, lambda k: l_across(c, k, 1 - core).wait_recv())
        rows = slice(c * 16, (c + 1) * 16)
        latents_out.append(pltpu.make_async_copy(lat.at[c], latents_hbm.at[:, :, rows], out_sem.at[c]))
        latents_out[c].start()

    def l_drain():
        for c in (0, 1):
            each(1, 8, lambda k: l_out(c, k).wait_send())
            each(0, 8, lambda k: l_across(c, k, core).wait_send())

    drains.append(l_drain)

    for drain in drains:
        drain()
    for copy in latents_out:
        copy.wait()
    steered_out.wait()


def local(
    new_queries, new_keys, new_values, key_cache, value_cache, cache_lengths, residual,
    output_weight, encoder_weight, encoder_bias, decoder_weight, decoder_bias, clamp_ids, clamp_values,
):
    hbm = pl.BlockSpec(memory_space=pl.ANY)
    V = pltpu.VMEM
    dma = pltpu.SemaphoreType.DMA
    steered, latents = pl.pallas_call(
        kernel,
        out_shape=(
            jax.ShapeDtypeStruct((32, 1024), BF16),
            jax.ShapeDtypeStruct((8, 2, 32, 1024), BF16),
        ),
        in_specs=[hbm] * 14,
        out_specs=(hbm, hbm),
        scratch_shapes=[
            V((16, 2048), BF16), V((16, 256, 128), BF16), V((16, 256, 128), BF16), V((32, 1024), BF16),
            V((2048, 1024), BF16), V((1024, 1024), BF16), V((1024, 1024), BF16),
            V((16, 128), BF16), V((16, 128), BF16), pltpu.SMEM((16,), jnp.int32), V((1, 1024), F32), V((1, 1024), F32),
            V((8, 512), jnp.int32), V((8, 512), jnp.int32),
            V((16, 16, 128), F32), V((16, 16, 128), F32),
            V((512, 8), F32), V((512, 8), F32), V((2, 16, 16, 1024), BF16), V((2, 16, 16, 1024), F32),
            V((16, 16, 1024), BF16), V((2, 16, 16, 128), BF16),
            V((8, 2, 16, 2048), BF16), V((2, 8, 16, 1024), F32), V((2, 8, 16, 1024), BF16), V((2, 8, 16, 1024), BF16),
            V((2, 16, 16, 1024), BF16), V((16, 16, 128), F32), V((16, 8, 128), F32),
            V((2, 8, 2, 16, 1024), F32), V((2, 8, 2, 16, 1024), BF16), V((2, 8, 16, 1024), BF16),
            V((2, 8, 16, 1024), BF16), V((2, 8, 16, 1024), BF16), V((2, 8, 2, 16, 1024), BF16),
            V((2, 16, 16, 1024), BF16), V((2, 16, 16, 1024), BF16), V((32, 1024), BF16),
            dma((14,)), dma((3,)),
            dma((8,)), dma((8,)), dma((8,)), dma((8,)), dma((2, 8)), dma((2, 8)),
            dma((2, 16)), dma((2, 16)), dma((16,)), dma((16,)), dma((16,)), dma((16,)),
            dma((2, 2)), dma((2, 2)), dma((2, 8)), dma((2, 8)), dma((2, 16)), dma((2, 16)),
            dma((2, 8)), dma((2, 8)), dma((2, 8)), dma((2, 8)), dma((2, 16)), dma((2, 16)),
        ],
        compiler_params=pltpu.CompilerParams(
            collective_id=0, has_side_effects=True, vmem_limit_bytes=62 * 2**20
        ),
    )(
        new_queries, new_keys, new_values, key_cache, value_cache, cache_lengths, residual,
        output_weight, encoder_weight, encoder_bias.reshape(1, 1024), decoder_weight,
        decoder_bias.reshape(1, 1024), clamp_ids.T, clamp_values.T,
    )
    return steered, latents.reshape(512, 1024)


def solution(mesh):
    in_specs = (
        P(("section", "feat"), "tensor"),
        P(("section", "feat"), "tensor"),
        P(("section", "feat"), "tensor"),
        P(("section", "feat"), None, "tensor"),
        P(("section", "feat"), None, "tensor"),
        P(("section", "feat")),
        P("section", "feat"),
        P("tensor", "feat"),
        P("feat", ("section", "tensor")),
        P(("section", "tensor")),
        P(("section", "tensor"), "feat"),
        P("feat"),
        P(),
        P(),
    )
    out_specs = (P(("section", "tensor"), "feat"), P(None, ("section", "tensor")))
    return jax.shard_map(local, mesh=mesh, in_specs=in_specs, out_specs=out_specs, check_vma=False)
```

```python
import functools
import math

import jax
import jax.numpy as jnp
from jax import lax
from jax.experimental import pallas as pl
from jax.experimental.pallas import tpu as pltpu
from jax.sharding import PartitionSpec as P

D = 16384
HD = 128
EPSILON = 1e-05
NEGATIVE = -1e30
MESH = pl.DeviceIdType.MESH
F32 = jnp.float32
BF16 = jnp.bfloat16

TILE = 256


def kernel(
    q_hbm, nk_hbm, nv_hbm, kc_hbm, vc_hbm, lens_hbm, res_hbm, wo_hbm, we_hbm,
    be_hbm, wd_hbm, bd_hbm, ids_hbm, vals_hbm,
    steered_hbm, latents_hbm,
    q_in, kc, vc, res, wo, we, wd, nk_ref, nv_ref, lens_ref, be_ref, bd_ref, ids_ref, vals_ref, q_heads, o_heads,
    keys_wide, values_wide, scores_all, weights,
    ids_col, vals_col, chosen, change, picked, current,
    att, proj, proj_send, proj_recv, hid, info, scales,
    enc, enc_send, pair_recv, z_send, enc_recv, lat, chg_send, f1_in, part, part_send, f2_in, out_rows,
    in_sem, out_sem,
    b_s, b_r, bp_s, bp_r, c_s, c_r, d1_s, d1_r, d2_s, d2_r, i_s, i_r, s_s, s_r,
    ep_s, ep_r, e_s, e_r, u_s, u_r, l_s, l_r, lp_s, lp_r, f1_s, f1_r, f2_s, f2_r,
):
    me_f = lax.axis_index("feat")
    me_t = lax.axis_index("tensor")
    me_a = lax.axis_index("section") * 8 + me_t
    z = me_f // 2
    core = lax.rem(me_f, 2)
    partner = me_f + 1 - 2 * core
    y, x = me_a // 4, lax.rem(me_a, 4)
    halves = (slice(0, 512), slice(512, 1024))

    def feat_id(f):
        return {"feat": f}

    def plane_id(a):
        return {"section": a // 8, "tensor": lax.rem(a, 8)}

    def each(first, last, do):
        def body(k, carry):
            do(k)
            return carry

        lax.fori_loop(first, last, body, 0)

    def push(src, dst, ss, rs, device):
        return pltpu.make_async_remote_copy(
            src_ref=src, dst_ref=dst, send_sem=ss, recv_sem=rs,
            device_id=device, device_id_type=MESH,
        )

    barrier = pltpu.get_barrier_semaphore()

    def announce(k):
        pl.semaphore_signal(barrier, inc=1, device_id=feat_id(lax.rem(me_f + k, 16)), device_id_type=MESH)
        pl.semaphore_signal(barrier, inc=1, device_id=plane_id(lax.rem(me_a + k, 16)), device_id_type=MESH)

    each(1, 16, announce)

    loads = [
        pltpu.make_async_copy(q_hbm, q_in, in_sem.at[0]),
        pltpu.make_async_copy(kc_hbm, kc, in_sem.at[1]),
        pltpu.make_async_copy(vc_hbm, vc, in_sem.at[2]),
        pltpu.make_async_copy(wo_hbm, wo, in_sem.at[3]),
        pltpu.make_async_copy(we_hbm, we, in_sem.at[4]),
        pltpu.make_async_copy(wd_hbm, wd, in_sem.at[5]),
        pltpu.make_async_copy(res_hbm.at[pl.ds(me_t * 32, 32)], res, in_sem.at[6]),
        pltpu.make_async_copy(nk_hbm, nk_ref, in_sem.at[7]),
        pltpu.make_async_copy(nv_hbm, nv_ref, in_sem.at[8]),
        pltpu.make_async_copy(lens_hbm, lens_ref, in_sem.at[9]),
        pltpu.make_async_copy(ids_hbm, ids_ref, in_sem.at[10]),
        pltpu.make_async_copy(vals_hbm, vals_ref, in_sem.at[11]),
        pltpu.make_async_copy(be_hbm, be_ref, in_sem.at[12]),
        pltpu.make_async_copy(bd_hbm, bd_ref, in_sem.at[13]),
    ]
    for i in (0, 7, 8, 9, 1, 2, 3, 10, 11, 6, 12, 13, 4, 5):
        loads[i].start()

    waited = set()

    def loaded(i):
        if i not in waited:
            waited.add(i)
            loads[i].wait()

    drains = []

    loaded(0)
    for h in range(16):
        q_heads[:, h, :] = q_in[:, h * HD : (h + 1) * HD].astype(F32)
    loaded(7)
    loaded(8)
    loaded(9)
    fresh_keys = nk_ref[...].astype(F32)
    fresh_values = nv_ref[...].astype(F32)
    loaded(1)
    loaded(2)
    score_scale = 1.0 / math.sqrt(HD)
    position = lax.broadcasted_iota(jnp.int32, (16, 256), 1)
    for r in range(16):
        keys_wide[r] = jnp.broadcast_to(fresh_keys[r : r + 1], (16, 128))
        values_wide[r] = jnp.broadcast_to(fresh_values[r : r + 1], (16, 128))
    for r in range(16):
        scores = lax.dot_general(
            q_heads[r].astype(BF16), kc[r], (((1,), (1,)), ((), ())), preferred_element_type=F32
        ) * score_scale
        scores_all[r] = jnp.where(position < lens_ref[r], scores, NEGATIVE)
    scores = scores_all[...]
    own_score = jnp.sum(q_heads[...] * keys_wide[...], -1, keepdims=True) * score_scale
    highest = jnp.maximum(jnp.max(scores, -1, keepdims=True), own_score)
    raw = jnp.exp(scores - highest)
    own_raw = jnp.exp(own_score - highest)
    totals = jnp.sum(raw, -1, keepdims=True) + own_raw
    weights[...] = raw.astype(BF16)
    for r in range(16):
        o_heads[r] = jnp.dot(weights[r], vc[r], preferred_element_type=F32)
    own_part = own_raw.astype(BF16).astype(F32) * values_wide[...]
    o_heads[...] = (o_heads[...] + own_part) * (1.0 / totals)
    for h in range(16):
        att[z, core, :, h * HD : (h + 1) * HD] = o_heads[:, h, :].astype(BF16)

    pl.semaphore_wait(barrier, 30)

    def b_out(k):
        return push(att.at[z, core], att.at[z, core], b_s.at[k], b_r.at[k], feat_id(lax.rem(me_f + 2 * k, 16)))

    def b_in(k):
        piece = att.at[lax.rem(z + 8 - k, 8), core]
        return push(piece, piece, b_s.at[k], b_r.at[k], feat_id(partner))

    def b_across(k, side):
        piece = att.at[lax.rem(z + 8 - k, 8), side]
        return push(piece, piece, bp_s.at[k], bp_r.at[k], feat_id(partner))

    each(1, 8, lambda k: b_out(k).start())
    b_across(0, core).start()

    loaded(10)
    loaded(11)
    ids_col[...] = ids_ref[...].astype(F32).T
    vals_col[...] = vals_ref[...].astype(F32).T
    first_latent = (me_a * 1024).astype(F32)

    def choose(i, carry):
        rows = pl.ds(pl.multiple_of(i * 32, 32), 32)
        ids = ids_col[rows, :] - first_latent
        values = vals_col[rows, :]
        column = lax.broadcasted_iota(jnp.int32, (32, 1024), 1).astype(F32)
        best = jnp.full((32, 1024), -1.0, F32)
        for j in range(8):
            best = jnp.where(ids[:, j : j + 1] == column, jnp.maximum(best, values[:, j : j + 1]), best)
        chosen[0, i] = best[0:16].astype(BF16)
        chosen[1, i] = best[16:32].astype(BF16)
        return carry

    lax.fori_loop(0, 16, choose, 0)

    def b_relay(k):
        b_in(k).wait_recv()
        b_across(k, core).start()

    for k in (1, 7, 2, 6, 3, 5, 4):
        b_relay(k)
    loaded(3)
    each(0, 8, lambda k: b_across(k, 1 - core).wait_recv())

    def b_drain():
        each(1, 8, lambda k: b_out(k).wait_send())
        each(0, 8, lambda k: b_across(k, core).wait_send())

    drains.append(b_drain)

    def tiles(do):
        for n in range(1024 // TILE):
            do(slice(n * TILE, (n + 1) * TILE))

    def c_push(c, k):
        peer = lax.rem(me_t + k, 8)
        return push(proj_send.at[c, peer], proj_recv.at[c, k], c_s.at[c, k], c_r.at[c, k], {"tensor": peer})

    def project(c):
        def tile(cols):
            term = jnp.dot(att[:, c].reshape(128, 2048), wo[:, cols], preferred_element_type=F32).reshape(8, 16, TILE)
            proj[c, :, :, cols] = term
            proj_send[c, :, :, cols] = term.astype(BF16)

        tiles(tile)
        each(1, 8, lambda k: c_push(c, k).start())
        drains.append(lambda: each(1, 8, lambda k: c_push(c, k).wait_send()))

    project(0)
    project(1)

    loaded(4)
    loaded(13)
    bias = bd_ref[...]
    high = bias.astype(BF16)
    rest = bias - high.astype(F32)
    middle = rest.astype(BF16)
    low = (rest - middle.astype(F32)).astype(BF16)
    index = lax.broadcasted_iota(jnp.int32, (16, 1024), 0)
    stacked = jnp.where(
        index == 0, high.astype(F32), jnp.where(index == 1, middle.astype(F32), jnp.where(index == 2, low.astype(F32), 0.0))
    ).astype(BF16)
    for n in range(4):
        term = jnp.dot(stacked, we[:, n * 256 : (n + 1) * 256], preferred_element_type=F32)
        term = jnp.sum(term[0:8], 0, keepdims=True)
        info[me_f, 2 * n : 2 * n + 1, :] = term[:, :128]
        info[me_f, 2 * n + 1 : 2 * n + 2, :] = term[:, 128:]

    loaded(6)

    def ring(place, step):
        return lax.rem(place + step + 4, 4)

    def d_first(c, h, k, arriving):
        yy, xx = (y, ring(x, -k if arriving else 0)) if h == 0 else (ring(y, -k if arriving else 0), x)
        peer = plane_id(y * 4 + ring(x, k)) if h == 0 else plane_id(ring(y, k) * 4 + x)
        piece = hid.at[c, yy, xx, :, halves[h]]
        return push(piece, piece, d1_s.at[c, h * 3 + k - 1], d1_r.at[c, h * 3 + k - 1], peer)

    def d_second(c, h, k, arriving):
        if h == 0:
            piece, peer = hid.at[c, ring(y, -k if arriving else 0), :, :, halves[0]], plane_id(ring(y, k) * 4 + x)
        else:
            piece, peer = hid.at[c, :, ring(x, -k if arriving else 0), :, halves[1]], plane_id(y * 4 + ring(x, k))
        return push(piece, piece, d2_s.at[c, h * 3 + k - 1], d2_r.at[c, h * 3 + k - 1], peer)

    def d_relay(c):
        for h in (0, 1):
            for k in (1, 3, 2):
                d_first(c, h, k, True).wait_recv()
            for k in (2, 1, 3):
                d_second(c, h, k, False).start()

    def d_drain():
        for c in (0, 1):
            for h in (0, 1):
                for k in (1, 2, 3):
                    d_first(c, h, k, False).wait_send()
                    d_second(c, h, k, False).wait_send()

    drains.append(d_drain)

    diagonal = lax.broadcasted_iota(jnp.int32, (32, 128), 0) == lax.broadcasted_iota(jnp.int32, (32, 128), 1)

    def hidden(c):
        total = proj[c, me_t] + res[c * 16 : (c + 1) * 16].astype(F32)
        for k in range(1, 8):
            c_push(c, k).wait_recv()
            total = total + proj_recv[c, k].astype(F32)
        total = total.astype(BF16)
        hid[c, y, x] = total
        for k in (2, 1, 3):
            d_first(c, 0, k, False).start()
            d_first(c, 1, k, False).start()
        wide = total.astype(F32)
        squares = wide * wide
        partial = squares[:, 0:128]
        for j in range(1, 8):
            partial = partial + squares[:, j * 128 : (j + 1) * 128]
        return jnp.sum(partial, -1, keepdims=True)

    sums = [hidden(0), hidden(1)]
    d_relay(0)
    d_relay(1)
    row = sum(jnp.sum(jnp.where(diagonal[16 * c : 16 * c + 16], sums[c], 0.0), 0, keepdims=True) for c in (0, 1))
    info[me_f, 8:16, :] = jnp.broadcast_to(row, (8, 128))

    def i_push(k):
        return push(info.at[me_f], info.at[me_f], i_s.at[k], i_r.at[k], feat_id(lax.rem(me_f + k, 16)))

    each(1, 16, lambda k: i_push(k).start())
    drains.append(lambda: each(1, 16, lambda k: i_push(k).wait_send()))

    loaded(5)

    def target_tile(c, cols):
        term = jnp.dot(jnp.maximum(chosen[c].reshape(256, 1024), 0), wd[:, cols], preferred_element_type=F32)
        change[c, :, :, :, cols] = term.reshape(4, 4, 16, TILE)

    tiles(lambda cols: target_tile(0, cols))
    tiles(lambda cols: target_tile(1, cols))

    def ep_push(c, n):
        cols = slice(n * 512, (n + 1) * 512)
        return push(
            enc_send.at[c, :, 1 - core, :, cols], pair_recv.at[c, :, :, cols],
            ep_s.at[c, n], ep_r.at[c, n], feat_id(partner),
        )

    def encode(c):
        for h in (0, 1):
            for k in (1, 3, 2):
                d_second(c, h, k, True).wait_recv()

        def tile(cols):
            term = jnp.dot(hid[c].reshape(256, 1024), we[:, cols], preferred_element_type=F32)
            term = term.reshape(8, 2, 16, TILE)
            enc[c, :, :, :, cols] = term
            enc_send[c, :, :, :, cols] = term.astype(BF16)
            if cols.stop % 512 == 0:
                ep_push(c, cols.stop // 512 - 1).start()

        tiles(tile)
        drains.append(lambda: [ep_push(c, n).wait_send() for n in (0, 1)])

    def e_push(c, k):
        peer = lax.rem(z + k, 8)
        return push(z_send.at[c, k], enc_recv.at[c, k], e_s.at[c, k], e_r.at[c, k], feat_id(peer * 2 + core))

    def exchange(c):
        for n in (0, 1):
            ep_push(c, n).wait_recv()

        def one(k):
            peer = lax.rem(z + k, 8)
            z_send[c, k] = (enc[c, peer, core] + pair_recv[c, peer].astype(F32)).astype(BF16)
            e_push(c, k).start()

        for k in (4, 3, 5, 2, 6, 1, 7):
            one(k)
        drains.append(lambda: each(1, 8, lambda k: e_push(c, k).wait_send()))

    encode(0)
    exchange(0)

    each(1, 16, lambda k: i_push(k).wait_recv())
    total_info = info[0]
    for f in range(1, 16):
        total_info = total_info + info[f]
    scales[me_a] = jnp.sqrt(total_info[8:16] / D + EPSILON)
    bias_term = total_info[0:8]

    def s_push(k):
        return push(scales.at[me_a], scales.at[me_a], s_s.at[k], s_r.at[k], plane_id(lax.rem(me_a + k, 16)))

    each(1, 16, lambda k: s_push(k).start())
    drains.append(lambda: each(1, 16, lambda k: s_push(k).wait_send()))

    def as_column(a):
        row = jnp.broadcast_to(scales[a, 0:1], (32, 128))
        return jnp.sum(jnp.where(diagonal, row, 0.0), -1, keepdims=True)

    encode(1)
    exchange(1)

    each(1, 16, lambda k: s_push(k).wait_recv())
    loaded(12)
    inverse = 1.0 / as_column(me_f)
    lane = lax.broadcasted_iota(jnp.int32, (16, 128), 1)
    column = lax.broadcasted_iota(jnp.int32, (16, 1024), 1).astype(F32)

    def row_ids(c, f):
        return ids_col[pl.ds(pl.multiple_of(f * 32 + c * 16, 16), 16), :] - first_latent

    def u_push(c, k):
        piece = current.at[c, me_f]
        return push(piece, piece, u_s.at[c, k], u_r.at[c, k], feat_id(lax.rem(me_f + k, 16)))

    def latents(c):
        total = enc[c, z, core] + pair_recv[c, z].astype(F32)
        for k in (1, 7, 2, 6, 3, 5, 4):
            e_push(c, k).wait_recv()
            total = total + enc_recv[c, k].astype(F32)
        scale = inverse[c * 16 : (c + 1) * 16]
        for j in range(8):
            cols = slice(j * 128, (j + 1) * 128)
            shift = be_ref[:, cols] - bias_term[j : j + 1]
            lat[c, z, core, :, cols] = jnp.maximum(total[:, cols] * scale + shift, 0.0).astype(BF16)
        mine = lat[c, z, core].astype(F32)
        ids = row_ids(c, me_f)
        held = jnp.zeros((16, 128), F32)
        for j in range(8):
            value = jnp.sum(jnp.where(ids[:, j : j + 1] == column, mine, 0.0), -1, keepdims=True)
            held = jnp.where(lane == j, value, held)
        current[c, me_f] = held.astype(BF16)
        each(1, 16, lambda k: u_push(c, k).start())
        drains.append(lambda: each(1, 16, lambda k: u_push(c, k).wait_send()))

    latents(0)
    latents(1)

    def l_out(c, k):
        piece = lat.at[c, z, core]
        return push(piece, piece, l_s.at[c, k], l_r.at[c, k], feat_id(lax.rem(me_f + 2 * k, 16)))

    def l_in(c, k):
        piece = lat.at[c, lax.rem(z + 8 - k, 8), core]
        return push(piece, piece, l_s.at[c, k], l_r.at[c, k], feat_id(partner))

    def l_across(c, k, side):
        piece = lat.at[c, lax.rem(z + 8 - k, 8), side]
        return push(piece, piece, lp_s.at[c, k], lp_r.at[c, k], feat_id(partner))

    for c in (0, 1):
        each(1, 8, lambda k: l_out(c, k).start())
        l_across(c, 0, core).start()

    def f_first(c, h, k):
        if h == 0:
            src, peer = chg_send.at[c, :, ring(x, k), :, halves[0]], plane_id(y * 4 + ring(x, k))
        else:
            src, peer = chg_send.at[c, ring(y, k), :, :, halves[1]], plane_id(ring(y, k) * 4 + x)
        return push(src, f1_in.at[c, h * 3 + k - 1], f1_s.at[c, h * 3 + k - 1], f1_r.at[c, h * 3 + k - 1], peer)

    def f_second(c, h, k):
        if h == 0:
            src, peer = part_send.at[c, 0, ring(y, k)], plane_id(ring(y, k) * 4 + x)
        else:
            src, peer = part_send.at[c, 1, ring(x, k)], plane_id(y * 4 + ring(x, k))
        return push(src, f2_in.at[c, h * 3 + k - 1], f2_s.at[c, h * 3 + k - 1], f2_r.at[c, h * 3 + k - 1], peer)

    def f_relay(c):
        for h in (0, 1):
            total = change[c, :, x, :, halves[0]] if h == 0 else change[c, y, :, :, halves[1]]
            for k in (1, 3, 2):
                f_first(c, h, k).wait_recv()
                total = total + f1_in[c, h * 3 + k - 1].astype(F32)
            part[c, h] = total
            part_send[c, h] = total.astype(BF16)
            for k in (2, 1, 3):
                f_second(c, h, k).start()

    def f_drain():
        for c in (0, 1):
            for h in (0, 1):
                for k in (1, 2, 3):
                    f_first(c, h, k).wait_send()
                    f_second(c, h, k).wait_send()

    def decode(c):
        each(1, 16, lambda k: u_push(c, k).wait_recv())

        def rebuild(f):
            ids = row_ids(c, f)
            values = current[c, f].astype(F32)
            best = jnp.zeros((16, 1024), F32)
            for j in range(8):
                best = jnp.where(ids[:, j : j + 1] == column, values[:, j : j + 1], best)
            picked[f] = best.astype(BF16)

        each(0, 16, rebuild)

        def tile(cols):
            term = jnp.dot(picked[...].reshape(256, 1024), wd[:, cols], preferred_element_type=F32)
            term = change[c, :, :, :, cols] - term.reshape(4, 4, 16, TILE)
            change[c, :, :, :, cols] = term
            chg_send[c, :, :, :, cols] = term.astype(BF16)
            if cols.stop % 512 == 0:
                for k in (2, 1, 3):
                    f_first(c, cols.stop // 512 - 1, k).start()

        tiles(tile)

    decode(0)
    decode(1)
    f_relay(0)
    f_relay(1)
    drains.append(f_drain)

    for c in (0, 1):
        for k in (1, 7, 2, 6, 3, 5, 4):
            l_in(c, k).wait_recv()
            l_across(c, k, core).start()

    own_scale = as_column(me_a)
    for c in (0, 1):
        rows = slice(c * 16, (c + 1) * 16)
        for h in (0, 1):
            total = part[c, h, y if h == 0 else x]
            for k in (1, 3, 2):
                f_second(c, h, k).wait_recv()
                total = total + f2_in[c, h * 3 + k - 1].astype(F32)
            own_hidden = hid[c, y, x, :, halves[h]].astype(F32)
            out_rows[rows, halves[h]] = (own_hidden + own_scale[rows] * total).astype(BF16)
    steered_out = pltpu.make_async_copy(out_rows, steered_hbm, out_sem.at[2])
    steered_out.start()

    latents_out = []
    for c in (0, 1):
        each(0, 8, lambda k: l_across(c, k, 1 - core).wait_recv())
        rows = slice(c * 16, (c + 1) * 16)
        latents_out.append(pltpu.make_async_copy(lat.at[c], latents_hbm.at[:, :, rows], out_sem.at[c]))
        latents_out[c].start()

    def l_drain():
        for c in (0, 1):
            each(1, 8, lambda k: l_out(c, k).wait_send())
            each(0, 8, lambda k: l_across(c, k, core).wait_send())

    drains.append(l_drain)

    for drain in drains:
        drain()
    for copy in latents_out:
        copy.wait()
    steered_out.wait()


def hand_over(steered_in, latents_in, steered, latents, rows_a, rows_b, sem_in, sem_out):
    steps = [(steered_in, rows_a, steered)]
    for i in range(4):
        rows = pl.ds(i * 128, 128)
        steps.append((latents_in.at[rows], rows_b.at[rows], latents.at[rows]))
    arriving = [pltpu.make_async_copy(a, b, sem_in.at[i]) for i, (a, b, _) in enumerate(steps)]
    leaving = [pltpu.make_async_copy(b, c, sem_out.at[i]) for i, (_, b, c) in enumerate(steps)]
    for copy in arriving:
        copy.start()
    for into, out in zip(arriving, leaving):
        into.wait()
        out.start()
    for copy in leaving:
        copy.wait()


def local(
    new_queries, new_keys, new_values, key_cache, value_cache, cache_lengths, residual,
    output_weight, encoder_weight, encoder_bias, decoder_weight, decoder_bias, clamp_ids, clamp_values,
):
    hbm = pl.BlockSpec(memory_space=pl.ANY)
    V = pltpu.VMEM
    dma = pltpu.SemaphoreType.DMA
    steered, latents = pl.pallas_call(
        kernel,
        out_shape=(
            jax.ShapeDtypeStruct((32, 1024), BF16),
            jax.ShapeDtypeStruct((8, 2, 32, 1024), BF16),
        ),
        in_specs=[hbm] * 14,
        out_specs=(hbm, hbm),
        scratch_shapes=[
            V((16, 2048), BF16), V((16, 256, 128), BF16), V((16, 256, 128), BF16), V((32, 1024), BF16),
            V((2048, 1024), BF16), V((1024, 1024), BF16), V((1024, 1024), BF16),
            V((16, 128), BF16), V((16, 128), BF16), pltpu.SMEM((16,), jnp.int32), V((1, 1024), F32), V((1, 1024), F32),
            V((8, 512), jnp.int32), V((8, 512), jnp.int32),
            V((16, 16, 128), F32), V((16, 16, 128), F32),
            V((16, 16, 128), F32), V((16, 16, 128), F32), V((16, 16, 256), F32), V((16, 16, 256), BF16),
            V((512, 8), F32), V((512, 8), F32), V((2, 16, 16, 1024), BF16), V((2, 4, 4, 16, 1024), F32),
            V((16, 16, 1024), BF16), V((2, 16, 16, 128), BF16),
            V((8, 2, 16, 2048), BF16), V((2, 8, 16, 1024), F32), V((2, 8, 16, 1024), BF16), V((2, 8, 16, 1024), BF16),
            V((2, 4, 4, 16, 1024), BF16), V((16, 16, 128), F32), V((16, 8, 128), F32),
            V((2, 8, 2, 16, 1024), F32), V((2, 8, 2, 16, 1024), BF16), V((2, 8, 16, 1024), BF16),
            V((2, 8, 16, 1024), BF16), V((2, 8, 16, 1024), BF16), V((2, 8, 2, 16, 1024), BF16),
            V((2, 4, 4, 16, 1024), BF16), V((2, 6, 4, 16, 512), BF16), V((2, 2, 4, 16, 512), F32),
            V((2, 2, 4, 16, 512), BF16), V((2, 6, 16, 512), BF16), V((32, 1024), BF16),
            dma((14,)), dma((3,)),
            dma((8,)), dma((8,)), dma((8,)), dma((8,)), dma((2, 8)), dma((2, 8)),
            dma((2, 6)), dma((2, 6)), dma((2, 6)), dma((2, 6)), dma((16,)), dma((16,)), dma((16,)), dma((16,)),
            dma((2, 2)), dma((2, 2)), dma((2, 8)), dma((2, 8)), dma((2, 16)), dma((2, 16)),
            dma((2, 8)), dma((2, 8)), dma((2, 8)), dma((2, 8)),
            dma((2, 6)), dma((2, 6)), dma((2, 6)), dma((2, 6)),
        ],
        compiler_params=pltpu.CompilerParams(
            collective_id=0, has_side_effects=True, vmem_limit_bytes=62 * 2**20
        ),
    )(
        new_queries, new_keys, new_values, key_cache, value_cache, cache_lengths, residual,
        output_weight, encoder_weight, encoder_bias.reshape(1, 1024), decoder_weight,
        decoder_bias.reshape(1, 1024), clamp_ids.T, clamp_values.T,
    )
    return pl.pallas_call(
        hand_over,
        out_shape=(jax.ShapeDtypeStruct((32, 1024), BF16), jax.ShapeDtypeStruct((512, 1024), BF16)),
        in_specs=[hbm, hbm],
        out_specs=(hbm, hbm),
        scratch_shapes=[V((32, 1024), BF16), V((512, 1024), BF16), dma((5,)), dma((5,))],
        compiler_params=pltpu.CompilerParams(vmem_limit_bytes=62 * 2**20),
    )(steered, latents.reshape(512, 1024))


def solution(mesh):
    in_specs = (
        P(("section", "feat"), "tensor"),
        P(("section", "feat"), "tensor"),
        P(("section", "feat"), "tensor"),
        P(("section", "feat"), None, "tensor"),
        P(("section", "feat"), None, "tensor"),
        P(("section", "feat")),
        P("section", "feat"),
        P("tensor", "feat"),
        P("feat", ("section", "tensor")),
        P(("section", "tensor")),
        P(("section", "tensor"), "feat"),
        P("feat"),
        P(),
        P(),
    )
    out_specs = (P(("section", "tensor"), "feat"), P(None, ("section", "tensor")))
    return jax.shard_map(local, mesh=mesh, in_specs=in_specs, out_specs=out_specs, check_vma=False)
```

```python
import functools
import math

import jax
import jax.numpy as jnp
from jax import lax
from jax.experimental import pallas as pl
from jax.experimental.pallas import tpu as pltpu
from jax.sharding import PartitionSpec as P

D = 16384
HD = 128
EPSILON = 1e-05
NEGATIVE = -1e30
MESH = pl.DeviceIdType.MESH
F32 = jnp.float32
BF16 = jnp.bfloat16

TILE = 256


def kernel(
    q_hbm, nk_hbm, nv_hbm, kc_hbm, vc_hbm, lens_hbm, res_hbm, wo_hbm, we_hbm,
    be_hbm, wd_hbm, bd_hbm, ids_hbm, vals_hbm,
    steered_hbm, latents_hbm,
    q_in, kc, vc, res, wo, we, wd, nk_ref, nv_ref, lens_ref, be_ref, bd_ref, ids_ref, vals_ref, q_heads, o_heads,
    keys_wide, values_wide, scores_all, weights,
    ids_col, vals_col, chosen, slots, change, picked, current,
    att, proj, proj_send, proj_recv, hid, info, scales,
    enc, enc_send, pair_recv, z_send, enc_recv, lat, chg_send, f1_in, part, part_send, f2_in, out_rows,
    in_sem, out_sem,
    b_s, b_r, bp_s, bp_r, c_s, c_r, d1_s, d1_r, d2_s, d2_r, i_s, i_r, s_s, s_r,
    ep_s, ep_r, e_s, e_r, u_s, u_r, l_s, l_r, lp_s, lp_r, f1_s, f1_r, f2_s, f2_r,
):
    me_f = lax.axis_index("feat")
    me_t = lax.axis_index("tensor")
    me_a = lax.axis_index("section") * 8 + me_t
    z = me_f // 2
    core = lax.rem(me_f, 2)
    partner = me_f + 1 - 2 * core
    y, x = me_a // 4, lax.rem(me_a, 4)
    halves = (slice(0, 512), slice(512, 1024))

    def feat_id(f):
        return {"feat": f}

    def plane_id(a):
        return {"section": a // 8, "tensor": lax.rem(a, 8)}

    def each(first, last, do):
        for k in range(first, last):
            do(k)

    def push(src, dst, ss, rs, device):
        return pltpu.make_async_remote_copy(
            src_ref=src, dst_ref=dst, send_sem=ss, recv_sem=rs,
            device_id=device, device_id_type=MESH,
        )

    loads = [
        pltpu.make_async_copy(q_hbm, q_in, in_sem.at[0]),
        pltpu.make_async_copy(kc_hbm, kc, in_sem.at[1]),
        pltpu.make_async_copy(vc_hbm, vc, in_sem.at[2]),
        pltpu.make_async_copy(wo_hbm, wo, in_sem.at[3]),
        pltpu.make_async_copy(we_hbm, we, in_sem.at[4]),
        pltpu.make_async_copy(wd_hbm, wd, in_sem.at[5]),
        pltpu.make_async_copy(res_hbm.at[pl.ds(me_t * 32, 32)], res, in_sem.at[6]),
        pltpu.make_async_copy(nk_hbm, nk_ref, in_sem.at[7]),
        pltpu.make_async_copy(nv_hbm, nv_ref, in_sem.at[8]),
        pltpu.make_async_copy(lens_hbm, lens_ref, in_sem.at[9]),
        pltpu.make_async_copy(ids_hbm, ids_ref, in_sem.at[10]),
        pltpu.make_async_copy(vals_hbm, vals_ref, in_sem.at[11]),
        pltpu.make_async_copy(be_hbm, be_ref, in_sem.at[12]),
        pltpu.make_async_copy(bd_hbm, bd_ref, in_sem.at[13]),
    ]
    for i in (0, 1, 2, 7, 8, 9, 10, 11):
        loads[i].start()

    barrier = pltpu.get_barrier_semaphore()

    def announce(k):
        pl.semaphore_signal(barrier, inc=1, device_id=feat_id(lax.rem(me_f + k, 16)), device_id_type=MESH)
        pl.semaphore_signal(barrier, inc=1, device_id=plane_id(lax.rem(me_a + k, 16)), device_id_type=MESH)

    each(1, 16, announce)

    waited = set()

    def loaded(i):
        if i not in waited:
            waited.add(i)
            loads[i].wait()

    drains = []

    loaded(0)
    for h in range(16):
        q_heads[:, h, :] = q_in[:, h * HD : (h + 1) * HD].astype(F32)
    loaded(7)
    loaded(8)
    loaded(9)
    fresh_keys = nk_ref[...].astype(F32)
    fresh_values = nv_ref[...].astype(F32)
    loaded(1)
    loaded(2)
    for i in (3, 6, 12, 13, 4, 5):
        loads[i].start()
    score_scale = 1.0 / math.sqrt(HD)
    position = lax.broadcasted_iota(jnp.int32, (16, 256), 1)
    for r in range(16):
        keys_wide[r] = jnp.broadcast_to(fresh_keys[r : r + 1], (16, 128))
        values_wide[r] = jnp.broadcast_to(fresh_values[r : r + 1], (16, 128))
    for r in range(16):
        scores = lax.dot_general(
            q_heads[r].astype(BF16), kc[r], (((1,), (1,)), ((), ())), preferred_element_type=F32
        ) * score_scale
        scores_all[r] = jnp.where(position < lens_ref[r], scores, NEGATIVE)
    scores = scores_all[...]
    own_score = jnp.sum(q_heads[...] * keys_wide[...], -1, keepdims=True) * score_scale
    highest = jnp.maximum(jnp.max(scores, -1, keepdims=True), own_score)
    raw = jnp.exp(scores - highest)
    own_raw = jnp.exp(own_score - highest)
    totals = jnp.sum(raw, -1, keepdims=True) + own_raw
    weights[...] = raw.astype(BF16)
    for r in range(16):
        o_heads[r] = jnp.dot(weights[r], vc[r], preferred_element_type=F32)
    own_part = own_raw.astype(BF16).astype(F32) * values_wide[...]
    o_heads[...] = (o_heads[...] + own_part) * (1.0 / totals)
    for h in range(16):
        att[z, core, :, h * HD : (h + 1) * HD] = o_heads[:, h, :].astype(BF16)

    pl.semaphore_wait(barrier, 30)

    GATHER = ((0, 2, None), (0, -2, None), (0, 1, None), (0, -1, None), (-2, 1, None), (2, -1, None), (-2, 2, 0), (2, -2, 1))

    def chip(step):
        return lax.rem(z + step + 8, 8)

    def columns(half, width):
        return slice(0, width) if half is None else slice(half * width // 2, (half + 1) * width // 2)

    def gather_z(buf, send, recv, across_send, across_recv):
        width = buf.shape[-1]

        def hop(slot, arriving):
            block, target, half = GATHER[slot]
            piece = buf.at[chip(block - target if arriving else block), core, :, columns(half, width)]
            return push(piece, piece, send(slot), recv(slot), feat_id(chip(target) * 2 + core))

        def across(slot, arriving):
            block, half = (0, None) if slot == 8 else (GATHER[slot][0] - GATHER[slot][1], GATHER[slot][2])
            piece = buf.at[chip(block), 1 - core if arriving else core, :, columns(half, width)]
            return push(piece, piece, across_send(slot), across_recv(slot), feat_id(partner))

        def start():
            for slot in range(4):
                hop(slot, False).start()
            across(8, False).start()

        def relay():
            for slot, follow in ((0, (6, 4)), (1, (7, 5))):
                hop(slot, True).wait_recv()
                for k in follow:
                    hop(k, False).start()

        def spread():
            for slot in (0, 1):
                across(slot, False).start()
            for slot in range(2, 8):
                hop(slot, True).wait_recv()
                across(slot, False).start()

        def finish():
            for slot in range(9):
                across(slot, True).wait_recv()

        def drain():
            for slot in range(8):
                hop(slot, False).wait_send()
            for slot in range(9):
                across(slot, False).wait_send()

        drains.append(drain)
        return start, relay, spread, finish

    b_start, b_relay, b_spread, b_finish = gather_z(
        att, lambda k: b_s.at[k], lambda k: b_r.at[k], lambda k: bp_s.at[k], lambda k: bp_r.at[k]
    )
    b_start()

    loaded(10)
    loaded(11)
    ids_col[...] = ids_ref[...].astype(F32).T
    vals_col[...] = vals_ref[...].astype(F32).T
    first_latent = (me_a * 1024).astype(F32)

    def choose(i, carry):
        rows = pl.ds(pl.multiple_of(i * 32, 32), 32)
        ids = ids_col[rows, :] - first_latent
        values = vals_col[rows, :]
        column = lax.broadcasted_iota(jnp.int32, (32, 1024), 1).astype(F32)
        best = jnp.full((32, 1024), -1.0, F32)
        slot = jnp.zeros((32, 1024), F32)
        for j in range(8):
            same = ids[:, j : j + 1] == column
            best = jnp.where(same, jnp.maximum(best, values[:, j : j + 1]), best)
            slot = jnp.where(same, j + 1.0, slot)
        chosen[0, i] = best[0:16].astype(BF16)
        chosen[1, i] = best[16:32].astype(BF16)
        slots[0, i] = slot[0:16].astype(BF16)
        slots[1, i] = slot[16:32].astype(BF16)
        return carry

    lax.fori_loop(0, 8, choose, 0)
    b_relay()
    lax.fori_loop(8, 16, choose, 0)
    b_spread()
    loaded(3)
    b_finish()

    def tiles(do):
        for n in range(1024 // TILE):
            do(slice(n * TILE, (n + 1) * TILE))

    def c_push(c, k):
        peer = lax.rem(me_t + k, 8)
        return push(proj_send.at[c, peer], proj_recv.at[c, k], c_s.at[c, k], c_r.at[c, k], {"tensor": peer})

    def project(c):
        def tile(cols):
            term = jnp.dot(att[:, c].reshape(128, 2048), wo[:, cols], preferred_element_type=F32).reshape(8, 16, TILE)
            proj[c, :, :, cols] = term
            proj_send[c, :, :, cols] = term.astype(BF16)

        tiles(tile)
        each(1, 8, lambda k: c_push(c, k).start())
        drains.append(lambda: each(1, 8, lambda k: c_push(c, k).wait_send()))

    project(0)
    project(1)

    loaded(4)
    loaded(13)
    bias = bd_ref[...]
    high = bias.astype(BF16)
    rest = bias - high.astype(F32)
    middle = rest.astype(BF16)
    low = (rest - middle.astype(F32)).astype(BF16)
    index = lax.broadcasted_iota(jnp.int32, (16, 1024), 0)
    stacked = jnp.where(
        index == 0, high.astype(F32), jnp.where(index == 1, middle.astype(F32), jnp.where(index == 2, low.astype(F32), 0.0))
    ).astype(BF16)
    for n in range(4):
        term = jnp.dot(stacked, we[:, n * 256 : (n + 1) * 256], preferred_element_type=F32)
        term = jnp.sum(term[0:8], 0, keepdims=True)
        info[me_f, 2 * n : 2 * n + 1, :] = term[:, :128]
        info[me_f, 2 * n + 1 : 2 * n + 2, :] = term[:, 128:]

    loaded(6)

    def ring(place, step):
        return lax.rem(place + step + 4, 4)

    def d_first(c, h, k, arriving):
        yy, xx = (y, ring(x, -k if arriving else 0)) if h == 0 else (ring(y, -k if arriving else 0), x)
        peer = plane_id(y * 4 + ring(x, k)) if h == 0 else plane_id(ring(y, k) * 4 + x)
        piece = hid.at[c, yy, xx, :, halves[h]]
        return push(piece, piece, d1_s.at[c, h * 3 + k - 1], d1_r.at[c, h * 3 + k - 1], peer)

    def d_second(c, h, k, arriving):
        if h == 0:
            piece, peer = hid.at[c, ring(y, -k if arriving else 0), :, :, halves[0]], plane_id(ring(y, k) * 4 + x)
        else:
            piece, peer = hid.at[c, :, ring(x, -k if arriving else 0), :, halves[1]], plane_id(y * 4 + ring(x, k))
        return push(piece, piece, d2_s.at[c, h * 3 + k - 1], d2_r.at[c, h * 3 + k - 1], peer)

    def d_relay(c):
        for h in (0, 1):
            for k in (1, 3, 2):
                d_first(c, h, k, True).wait_recv()
            for k in (2, 1, 3):
                d_second(c, h, k, False).start()

    def d_drain():
        for c in (0, 1):
            for h in (0, 1):
                for k in (1, 2, 3):
                    d_first(c, h, k, False).wait_send()
                    d_second(c, h, k, False).wait_send()

    drains.append(d_drain)

    diagonal = lax.broadcasted_iota(jnp.int32, (32, 128), 0) == lax.broadcasted_iota(jnp.int32, (32, 128), 1)

    def hidden(c):
        total = proj[c, me_t] + res[c * 16 : (c + 1) * 16].astype(F32)
        for k in range(1, 8):
            c_push(c, k).wait_recv()
            total = total + proj_recv[c, k].astype(F32)
        total = total.astype(BF16)
        hid[c, y, x] = total
        for k in (2, 1, 3):
            d_first(c, 0, k, False).start()
            d_first(c, 1, k, False).start()
        wide = total.astype(F32)
        squares = wide * wide
        partial = squares[:, 0:128]
        for j in range(1, 8):
            partial = partial + squares[:, j * 128 : (j + 1) * 128]
        return jnp.sum(partial, -1, keepdims=True)

    sums = [hidden(0), hidden(1)]
    d_relay(0)
    d_relay(1)
    row = sum(jnp.sum(jnp.where(diagonal[16 * c : 16 * c + 16], sums[c], 0.0), 0, keepdims=True) for c in (0, 1))
    info[me_f, 8:16, :] = jnp.broadcast_to(row, (8, 128))

    def i_push(k):
        return push(info.at[me_f], info.at[me_f], i_s.at[k], i_r.at[k], feat_id(lax.rem(me_f + k, 16)))

    each(1, 16, lambda k: i_push(k).start())
    drains.append(lambda: each(1, 16, lambda k: i_push(k).wait_send()))

    loaded(5)

    def target_tile(c, cols):
        term = jnp.dot(jnp.maximum(chosen[c].reshape(256, 1024), 0), wd[:, cols], preferred_element_type=F32)
        change[c, :, :, :, cols] = term.reshape(4, 4, 16, TILE)

    tiles(lambda cols: target_tile(0, cols))
    tiles(lambda cols: target_tile(1, cols))

    def ep_push(c, n):
        cols = slice(n * 512, (n + 1) * 512)
        return push(
            enc_send.at[c, :, 1 - core, :, cols], pair_recv.at[c, :, :, cols],
            ep_s.at[c, n], ep_r.at[c, n], feat_id(partner),
        )

    def encode(c):
        for h in (0, 1):
            for k in (1, 3, 2):
                d_second(c, h, k, True).wait_recv()

        def tile(cols):
            term = jnp.dot(hid[c].reshape(256, 1024), we[:, cols], preferred_element_type=F32)
            term = term.reshape(8, 2, 16, TILE)
            enc[c, :, :, :, cols] = term
            enc_send[c, :, :, :, cols] = term.astype(BF16)
            if cols.stop % 512 == 0:
                ep_push(c, cols.stop // 512 - 1).start()

        tiles(tile)
        drains.append(lambda: [ep_push(c, n).wait_send() for n in (0, 1)])

    SUMS = ((4, 2, 0), (-4, -2, 1), (3, 1, None), (-3, -1, None), (1, 1, None), (-1, -1, None), (2, 2, None), (-2, -2, None))

    def e_push(c, slot):
        _, target, half = SUMS[slot]
        cols = columns(half, 1024)
        return push(
            z_send.at[c, slot, :, cols], enc_recv.at[c, slot, :, cols], e_s.at[c, slot], e_r.at[c, slot],
            feat_id(chip(target) * 2 + core),
        )

    def e_part(c, slot):
        final, _, half = SUMS[slot]
        cols = columns(half, 1024)
        return enc[c, chip(final), core, :, cols] + pair_recv[c, chip(final), :, cols].astype(F32)

    def exchange(c):
        for n in (0, 1):
            ep_push(c, n).wait_recv()
        for slot in range(6):
            z_send[c, slot, :, columns(SUMS[slot][2], 1024)] = e_part(c, slot).astype(BF16)
            e_push(c, slot).start()

    def e_relay(c):
        for slot, near, half in ((6, 2, 0), (7, 3, 1)):
            e_push(c, near).wait_recv()
            e_push(c, half).wait_recv()
            total = e_part(c, slot) + enc_recv[c, near].astype(F32)
            cols, rest = columns(half, 1024), columns(1 - half, 1024)
            z_send[c, slot, :, cols] = (total[:, cols] + enc_recv[c, half, :, cols].astype(F32)).astype(BF16)
            z_send[c, slot, :, rest] = total[:, rest].astype(BF16)
            e_push(c, slot).start()
        drains.append(lambda: each(0, 8, lambda slot: e_push(c, slot).wait_send()))

    encode(0)
    exchange(0)

    each(1, 16, lambda k: i_push(k).wait_recv())
    total_info = info[0]
    for f in range(1, 16):
        total_info = total_info + info[f]
    scales[me_a] = jnp.sqrt(total_info[8:16] / D + EPSILON)
    bias_term = total_info[0:8]

    def s_push(k):
        return push(scales.at[me_a], scales.at[me_a], s_s.at[k], s_r.at[k], plane_id(lax.rem(me_a + k, 16)))

    each(1, 16, lambda k: s_push(k).start())
    drains.append(lambda: each(1, 16, lambda k: s_push(k).wait_send()))

    def as_column(a):
        row = jnp.broadcast_to(scales[a, 0:1], (32, 128))
        return jnp.sum(jnp.where(diagonal, row, 0.0), -1, keepdims=True)

    encode(1)
    e_relay(0)
    exchange(1)
    e_relay(1)

    each(1, 16, lambda k: s_push(k).wait_recv())
    loaded(12)
    inverse = 1.0 / as_column(me_f)
    lane = lax.broadcasted_iota(jnp.int32, (16, 128), 1)
    column = lax.broadcasted_iota(jnp.int32, (16, 1024), 1).astype(F32)

    def row_ids(c, f):
        return ids_col[pl.ds(pl.multiple_of(f * 32 + c * 16, 16), 16), :] - first_latent

    def u_push(c, k):
        piece = current.at[c, me_f]
        return push(piece, piece, u_s.at[c, k], u_r.at[c, k], feat_id(lax.rem(me_f + k, 16)))

    def latents(c):
        total = enc[c, z, core] + pair_recv[c, z].astype(F32)
        for k in (4, 5, 6, 7):
            e_push(c, k).wait_recv()
            total = total + enc_recv[c, k].astype(F32)
        scale = inverse[c * 16 : (c + 1) * 16]
        for j in range(8):
            cols = slice(j * 128, (j + 1) * 128)
            shift = be_ref[:, cols] - bias_term[j : j + 1]
            lat[c, z, core, :, cols] = jnp.maximum(total[:, cols] * scale + shift, 0.0).astype(BF16)
        mine = lat[c, z, core].astype(F32)
        ids = row_ids(c, me_f)
        held = jnp.zeros((16, 128), F32)
        for j in range(8):
            value = jnp.sum(jnp.where(ids[:, j : j + 1] == column, mine, 0.0), -1, keepdims=True)
            held = jnp.where(lane == j, value, held)
        current[c, me_f] = held.astype(BF16)
        each(1, 16, lambda k: u_push(c, k).start())
        drains.append(lambda: each(1, 16, lambda k: u_push(c, k).wait_send()))

    latents(0)
    latents(1)

    gathers = [
        gather_z(
            lat.at[c], lambda k, c=c: l_s.at[c, k], lambda k, c=c: l_r.at[c, k],
            lambda k, c=c: lp_s.at[c, k], lambda k, c=c: lp_r.at[c, k],
        )
        for c in (0, 1)
    ]
    for c in (0, 1):
        gathers[c][0]()

    def f_first(c, h, k):
        if h == 0:
            src, peer = chg_send.at[c, :, ring(x, k), :, halves[0]], plane_id(y * 4 + ring(x, k))
        else:
            src, peer = chg_send.at[c, ring(y, k), :, :, halves[1]], plane_id(ring(y, k) * 4 + x)
        return push(src, f1_in.at[c, h * 3 + k - 1], f1_s.at[c, h * 3 + k - 1], f1_r.at[c, h * 3 + k - 1], peer)

    def f_second(c, h, k):
        if h == 0:
            src, peer = part_send.at[c, 0, ring(y, k)], plane_id(ring(y, k) * 4 + x)
        else:
            src, peer = part_send.at[c, 1, ring(x, k)], plane_id(y * 4 + ring(x, k))
        return push(src, f2_in.at[c, h * 3 + k - 1], f2_s.at[c, h * 3 + k - 1], f2_r.at[c, h * 3 + k - 1], peer)

    def f_relay(c):
        for h in (0, 1):
            total = change[c, :, x, :, halves[0]] if h == 0 else change[c, y, :, :, halves[1]]
            for k in (1, 3, 2):
                f_first(c, h, k).wait_recv()
                total = total + f1_in[c, h * 3 + k - 1].astype(F32)
            part[c, h] = total
            part_send[c, h] = total.astype(BF16)
            for k in (2, 1, 3):
                f_second(c, h, k).start()

    def f_drain():
        for c in (0, 1):
            for h in (0, 1):
                for k in (1, 2, 3):
                    f_first(c, h, k).wait_send()
                    f_second(c, h, k).wait_send()

    def decode(c):
        each(1, 16, lambda k: u_push(c, k).wait_recv())

        def rebuild(f):
            slot = slots[c, f].astype(F32)
            values = current[c, f].astype(F32)
            best = jnp.zeros((16, 1024), F32)
            for j in range(8):
                best = jnp.where(slot == j + 1, values[:, j : j + 1], best)
            picked[f] = best.astype(BF16)

        each(0, 16, rebuild)

        def tile(cols):
            term = jnp.dot(picked[...].reshape(256, 1024), wd[:, cols], preferred_element_type=F32)
            term = change[c, :, :, :, cols] - term.reshape(4, 4, 16, TILE)
            change[c, :, :, :, cols] = term
            chg_send[c, :, :, :, cols] = term.astype(BF16)
            if cols.stop % 512 == 0:
                for k in (2, 1, 3):
                    f_first(c, cols.stop // 512 - 1, k).start()

        tiles(tile)

    decode(0)
    decode(1)
    for c in (0, 1):
        gathers[c][1]()
    f_relay(0)
    f_relay(1)
    drains.append(f_drain)

    for c in (0, 1):
        gathers[c][2]()

    own_scale = as_column(me_a)
    for c in (0, 1):
        rows = slice(c * 16, (c + 1) * 16)
        for h in (0, 1):
            total = part[c, h, y if h == 0 else x]
            for k in (1, 3, 2):
                f_second(c, h, k).wait_recv()
                total = total + f2_in[c, h * 3 + k - 1].astype(F32)
            own_hidden = hid[c, y, x, :, halves[h]].astype(F32)
            out_rows[rows, halves[h]] = (own_hidden + own_scale[rows] * total).astype(BF16)
    steered_out = pltpu.make_async_copy(out_rows, steered_hbm, out_sem.at[2])
    steered_out.start()

    latents_out = []
    for c in (0, 1):
        gathers[c][3]()
        rows = slice(c * 16, (c + 1) * 16)
        latents_out.append(pltpu.make_async_copy(lat.at[c], latents_hbm.at[:, :, rows], out_sem.at[c]))
        latents_out[c].start()

    for drain in drains:
        drain()
    for copy in latents_out:
        copy.wait()
    steered_out.wait()


def hand_over(steered_in, latents_in, steered, latents, rows_a, rows_b, sem_in, sem_out):
    steps = [(steered_in, rows_a, steered)]
    for i in range(4):
        rows = pl.ds(i * 128, 128)
        steps.append((latents_in.at[rows], rows_b.at[rows], latents.at[rows]))
    arriving = [pltpu.make_async_copy(a, b, sem_in.at[i]) for i, (a, b, _) in enumerate(steps)]
    leaving = [pltpu.make_async_copy(b, c, sem_out.at[i]) for i, (_, b, c) in enumerate(steps)]
    for copy in arriving:
        copy.start()
    for into, out in zip(arriving, leaving):
        into.wait()
        out.start()
    for copy in leaving:
        copy.wait()


def local(
    new_queries, new_keys, new_values, key_cache, value_cache, cache_lengths, residual,
    output_weight, encoder_weight, encoder_bias, decoder_weight, decoder_bias, clamp_ids, clamp_values,
):
    hbm = pl.BlockSpec(memory_space=pl.ANY)
    V = pltpu.VMEM
    dma = pltpu.SemaphoreType.DMA
    steered, latents = pl.pallas_call(
        kernel,
        out_shape=(
            jax.ShapeDtypeStruct((32, 1024), BF16),
            jax.ShapeDtypeStruct((8, 2, 32, 1024), BF16),
        ),
        in_specs=[hbm] * 14,
        out_specs=(hbm, hbm),
        scratch_shapes=[
            V((16, 2048), BF16), V((16, 256, 128), BF16), V((16, 256, 128), BF16), V((32, 1024), BF16),
            V((2048, 1024), BF16), V((1024, 1024), BF16), V((1024, 1024), BF16),
            V((16, 128), BF16), V((16, 128), BF16), pltpu.SMEM((16,), jnp.int32), V((1, 1024), F32), V((1, 1024), F32),
            V((8, 512), jnp.int32), V((8, 512), jnp.int32),
            V((16, 16, 128), F32), V((16, 16, 128), F32),
            V((16, 16, 128), F32), V((16, 16, 128), F32), V((16, 16, 256), F32), V((16, 16, 256), BF16),
            V((512, 8), F32), V((512, 8), F32), V((2, 16, 16, 1024), BF16), V((2, 16, 16, 1024), BF16),
            V((2, 4, 4, 16, 1024), F32),
            V((16, 16, 1024), BF16), V((2, 16, 16, 128), BF16),
            V((8, 2, 16, 2048), BF16), V((2, 8, 16, 1024), F32), V((2, 8, 16, 1024), BF16), V((2, 8, 16, 1024), BF16),
            V((2, 4, 4, 16, 1024), BF16), V((16, 16, 128), F32), V((16, 8, 128), F32),
            V((2, 8, 2, 16, 1024), F32), V((2, 8, 2, 16, 1024), BF16), V((2, 8, 16, 1024), BF16),
            V((2, 8, 16, 1024), BF16), V((2, 8, 16, 1024), BF16), V((2, 8, 2, 16, 1024), BF16),
            V((2, 4, 4, 16, 1024), BF16), V((2, 6, 4, 16, 512), BF16), V((2, 2, 4, 16, 512), F32),
            V((2, 2, 4, 16, 512), BF16), V((2, 6, 16, 512), BF16), V((32, 1024), BF16),
            dma((14,)), dma((3,)),
            dma((8,)), dma((8,)), dma((9,)), dma((9,)), dma((2, 8)), dma((2, 8)),
            dma((2, 6)), dma((2, 6)), dma((2, 6)), dma((2, 6)), dma((16,)), dma((16,)), dma((16,)), dma((16,)),
            dma((2, 2)), dma((2, 2)), dma((2, 8)), dma((2, 8)), dma((2, 16)), dma((2, 16)),
            dma((2, 8)), dma((2, 8)), dma((2, 9)), dma((2, 9)),
            dma((2, 6)), dma((2, 6)), dma((2, 6)), dma((2, 6)),
        ],
        compiler_params=pltpu.CompilerParams(
            collective_id=0, has_side_effects=True, vmem_limit_bytes=62 * 2**20
        ),
    )(
        new_queries, new_keys, new_values, key_cache, value_cache, cache_lengths, residual,
        output_weight, encoder_weight, encoder_bias.reshape(1, 1024), decoder_weight,
        decoder_bias.reshape(1, 1024), clamp_ids.T, clamp_values.T,
    )
    return pl.pallas_call(
        hand_over,
        out_shape=(jax.ShapeDtypeStruct((32, 1024), BF16), jax.ShapeDtypeStruct((512, 1024), BF16)),
        in_specs=[hbm, hbm],
        out_specs=(hbm, hbm),
        scratch_shapes=[V((32, 1024), BF16), V((512, 1024), BF16), dma((5,)), dma((5,))],
        compiler_params=pltpu.CompilerParams(vmem_limit_bytes=62 * 2**20),
    )(steered, latents.reshape(512, 1024))


def solution(mesh):
    in_specs = (
        P(("section", "feat"), "tensor"),
        P(("section", "feat"), "tensor"),
        P(("section", "feat"), "tensor"),
        P(("section", "feat"), None, "tensor"),
        P(("section", "feat"), None, "tensor"),
        P(("section", "feat")),
        P("section", "feat"),
        P("tensor", "feat"),
        P("feat", ("section", "tensor")),
        P(("section", "tensor")),
        P(("section", "tensor"), "feat"),
        P("feat"),
        P(),
        P(),
    )
    out_specs = (P(("section", "tensor"), "feat"), P(None, ("section", "tensor")))
    return jax.shard_map(local, mesh=mesh, in_specs=in_specs, out_specs=out_specs, check_vma=False)
```

```python
import functools
import math

import jax
import jax.numpy as jnp
from jax import lax
from jax.experimental import pallas as pl
from jax.experimental.pallas import tpu as pltpu
from jax.sharding import PartitionSpec as P

D = 16384
HD = 128
EPSILON = 1e-05
NEGATIVE = -1e30
MESH = pl.DeviceIdType.MESH
F32 = jnp.float32
BF16 = jnp.bfloat16

TILE = 256


def kernel(
    q_hbm, nk_hbm, nv_hbm, kc_hbm, vc_hbm, lens_hbm, res_hbm, wo_hbm, we_hbm,
    be_hbm, wd_hbm, bd_hbm, ids_hbm, vals_hbm,
    steered_hbm, latents_hbm,
    q_in, kc, vc, res, wo, we, wd, nk_ref, nv_ref, lens_ref, be_ref, bd_ref, ids_ref, vals_ref, q_heads, o_heads,
    keys_wide, values_wide, scores_all, weights,
    ids_col, vals_col, chosen, slots, change, picked, current,
    att, proj, proj_send, proj_recv, hid, info, scales,
    enc, enc_send, pair_recv, z_send, enc_recv, lat, chg_send, f1_in, part, part_send, f2_in, out_rows,
    in_sem, out_sem,
    b_s, b_r, bp_s, bp_r, c_s, c_r, d1_s, d1_r, d2_s, d2_r, i_s, i_r, s_s, s_r,
    ep_s, ep_r, e_s, e_r, u_s, u_r, l_s, l_r, lp_s, lp_r, f1_s, f1_r, f2_s, f2_r,
):
    me_f = lax.axis_index("feat")
    me_t = lax.axis_index("tensor")
    me_a = lax.axis_index("section") * 8 + me_t
    z = me_f // 2
    core = lax.rem(me_f, 2)
    partner = me_f + 1 - 2 * core
    y, x = me_a // 4, lax.rem(me_a, 4)
    halves = (slice(0, 512), slice(512, 1024))

    def feat_id(f):
        return {"feat": f}

    def plane_id(a):
        return {"section": a // 8, "tensor": lax.rem(a, 8)}

    def each(first, last, do):
        for k in range(first, last):
            do(k)

    def push(src, dst, ss, rs, device):
        return pltpu.make_async_remote_copy(
            src_ref=src, dst_ref=dst, send_sem=ss, recv_sem=rs,
            device_id=device, device_id_type=MESH,
        )

    loads = [
        pltpu.make_async_copy(q_hbm, q_in, in_sem.at[0]),
        pltpu.make_async_copy(kc_hbm, kc, in_sem.at[1]),
        pltpu.make_async_copy(vc_hbm, vc, in_sem.at[2]),
        pltpu.make_async_copy(wo_hbm, wo, in_sem.at[3]),
        pltpu.make_async_copy(we_hbm, we, in_sem.at[4]),
        pltpu.make_async_copy(wd_hbm, wd, in_sem.at[5]),
        pltpu.make_async_copy(res_hbm.at[pl.ds(me_t * 32, 32)], res, in_sem.at[6]),
        pltpu.make_async_copy(nk_hbm, nk_ref, in_sem.at[7]),
        pltpu.make_async_copy(nv_hbm, nv_ref, in_sem.at[8]),
        pltpu.make_async_copy(lens_hbm, lens_ref, in_sem.at[9]),
        pltpu.make_async_copy(ids_hbm, ids_ref, in_sem.at[10]),
        pltpu.make_async_copy(vals_hbm, vals_ref, in_sem.at[11]),
        pltpu.make_async_copy(be_hbm, be_ref, in_sem.at[12]),
        pltpu.make_async_copy(bd_hbm, bd_ref, in_sem.at[13]),
    ]
    for i in (0, 1, 2, 7, 8, 9, 10, 11):
        loads[i].start()

    barrier = pltpu.get_barrier_semaphore()

    def announce(k):
        pl.semaphore_signal(barrier, inc=1, device_id=feat_id(lax.rem(me_f + k, 16)), device_id_type=MESH)
        pl.semaphore_signal(barrier, inc=1, device_id=plane_id(lax.rem(me_a + k, 16)), device_id_type=MESH)

    each(1, 16, announce)

    waited = set()

    def loaded(i):
        if i not in waited:
            waited.add(i)
            loads[i].wait()

    drains = []

    loaded(0)
    for h in range(16):
        q_heads[:, h, :] = q_in[:, h * HD : (h + 1) * HD].astype(F32)
    loaded(7)
    loaded(8)
    loaded(9)
    fresh_keys = nk_ref[...].astype(F32)
    fresh_values = nv_ref[...].astype(F32)
    loaded(1)
    loaded(2)
    for i in (3, 6, 12, 13, 4, 5):
        loads[i].start()
    score_scale = 1.0 / math.sqrt(HD)
    position = lax.broadcasted_iota(jnp.int32, (16, 256), 1)
    for r in range(16):
        keys_wide[r] = jnp.broadcast_to(fresh_keys[r : r + 1], (16, 128))
        values_wide[r] = jnp.broadcast_to(fresh_values[r : r + 1], (16, 128))
    for r in range(16):
        scores = lax.dot_general(
            q_heads[r].astype(BF16), kc[r], (((1,), (1,)), ((), ())), preferred_element_type=F32
        ) * score_scale
        scores_all[r] = jnp.where(position < lens_ref[r], scores, NEGATIVE)
    scores = scores_all[...]
    own_score = jnp.sum(q_heads[...] * keys_wide[...], -1, keepdims=True) * score_scale
    highest = jnp.maximum(jnp.max(scores, -1, keepdims=True), own_score)
    raw = jnp.exp(scores - highest)
    own_raw = jnp.exp(own_score - highest)
    totals = jnp.sum(raw, -1, keepdims=True) + own_raw
    weights[...] = raw.astype(BF16)
    for r in range(16):
        o_heads[r] = jnp.dot(weights[r], vc[r], preferred_element_type=F32)
    own_part = own_raw.astype(BF16).astype(F32) * values_wide[...]
    o_heads[...] = (o_heads[...] + own_part) * (1.0 / totals)
    for h in range(16):
        att[z, core, :, h * HD : (h + 1) * HD] = o_heads[:, h, :].astype(BF16)

    pl.semaphore_wait(barrier, 30)

    GATHER = ((0, 2, None), (0, -2, None), (0, 1, None), (0, -1, None), (-2, 1, None), (2, -1, None), (-2, 2, 0), (2, -2, 1))

    def chip(step):
        return lax.rem(z + step + 8, 8)

    def columns(half, width):
        return slice(0, width) if half is None else slice(half * width // 2, (half + 1) * width // 2)

    def gather_z(buf, send, recv, across_send, across_recv):
        width = buf.shape[-1]

        def hop(slot, arriving):
            block, target, half = GATHER[slot]
            piece = buf.at[chip(block - target if arriving else block), core, :, columns(half, width)]
            return push(piece, piece, send(slot), recv(slot), feat_id(chip(target) * 2 + core))

        def across(slot, arriving):
            block, half = (0, None) if slot == 8 else (GATHER[slot][0] - GATHER[slot][1], GATHER[slot][2])
            piece = buf.at[chip(block), 1 - core if arriving else core, :, columns(half, width)]
            return push(piece, piece, across_send(slot), across_recv(slot), feat_id(partner))

        def start():
            for slot in range(4):
                hop(slot, False).start()
            across(8, False).start()

        def relay():
            for slot, follow in ((0, (6, 4)), (1, (7, 5))):
                hop(slot, True).wait_recv()
                for k in follow:
                    hop(k, False).start()

        def spread():
            for slot in (0, 1):
                across(slot, False).start()
            for slot in range(2, 8):
                hop(slot, True).wait_recv()
                across(slot, False).start()

        def finish():
            for slot in range(9):
                across(slot, True).wait_recv()

        def drain():
            for slot in range(8):
                hop(slot, False).wait_send()
            for slot in range(9):
                across(slot, False).wait_send()

        drains.append(drain)
        return start, relay, spread, finish

    b_start, b_relay, b_spread, b_finish = gather_z(
        att, lambda k: b_s.at[k], lambda k: b_r.at[k], lambda k: bp_s.at[k], lambda k: bp_r.at[k]
    )
    b_start()

    loaded(10)
    loaded(11)
    ids_col[...] = ids_ref[...].astype(F32).T
    vals_col[...] = vals_ref[...].astype(F32).T
    first_latent = (me_a * 1024).astype(F32)

    def choose(i, carry):
        rows = pl.ds(pl.multiple_of(i * 32, 32), 32)
        ids = ids_col[rows, :] - first_latent
        values = vals_col[rows, :]
        column = lax.broadcasted_iota(jnp.int32, (32, 1024), 1).astype(F32)
        best = jnp.full((32, 1024), -1.0, F32)
        slot = jnp.zeros((32, 1024), F32)
        for j in range(8):
            same = ids[:, j : j + 1] == column
            best = jnp.where(same, jnp.maximum(best, values[:, j : j + 1]), best)
            slot = jnp.where(same, j + 1.0, slot)
        chosen[0, i] = best[0:16].astype(BF16)
        chosen[1, i] = best[16:32].astype(BF16)
        slots[0, i] = slot[0:16].astype(BF16)
        slots[1, i] = slot[16:32].astype(BF16)
        return carry

    lax.fori_loop(0, 8, choose, 0)
    b_relay()
    lax.fori_loop(8, 16, choose, 0)
    b_spread()
    loaded(3)
    b_finish()

    def tiles(do):
        for n in range(1024 // TILE):
            do(slice(n * TILE, (n + 1) * TILE))

    def c_push(c, k):
        peer = lax.rem(me_t + k, 8)
        return push(proj_send.at[c, peer], proj_recv.at[c, k], c_s.at[c, k], c_r.at[c, k], {"tensor": peer})

    def project(c):
        def tile(cols):
            term = jnp.dot(att[:, c].reshape(128, 2048), wo[:, cols], preferred_element_type=F32).reshape(8, 16, TILE)
            proj[c, :, :, cols] = term
            proj_send[c, :, :, cols] = term.astype(BF16)

        tiles(tile)
        each(1, 8, lambda k: c_push(c, k).start())
        drains.append(lambda: each(1, 8, lambda k: c_push(c, k).wait_send()))

    project(0)
    project(1)

    loaded(4)
    loaded(13)
    bias = bd_ref[...]
    high = bias.astype(BF16)
    rest = bias - high.astype(F32)
    middle = rest.astype(BF16)
    low = (rest - middle.astype(F32)).astype(BF16)
    index = lax.broadcasted_iota(jnp.int32, (16, 1024), 0)
    stacked = jnp.where(
        index == 0, high.astype(F32), jnp.where(index == 1, middle.astype(F32), jnp.where(index == 2, low.astype(F32), 0.0))
    ).astype(BF16)
    for n in range(4):
        term = jnp.dot(stacked, we[:, n * 256 : (n + 1) * 256], preferred_element_type=F32)
        term = jnp.sum(term[0:8], 0, keepdims=True)
        info[me_f, 2 * n : 2 * n + 1, :] = term[:, :128]
        info[me_f, 2 * n + 1 : 2 * n + 2, :] = term[:, 128:]

    loaded(6)

    def ring(place, step):
        return lax.rem(place + step + 4, 4)

    def d_first(c, h, k, arriving):
        yy, xx = (y, ring(x, -k if arriving else 0)) if h == 0 else (ring(y, -k if arriving else 0), x)
        peer = plane_id(y * 4 + ring(x, k)) if h == 0 else plane_id(ring(y, k) * 4 + x)
        piece = hid.at[c, yy, xx, :, halves[h]]
        return push(piece, piece, d1_s.at[c, h * 3 + k - 1], d1_r.at[c, h * 3 + k - 1], peer)

    def d_second(c, h, k, arriving):
        if h == 0:
            piece, peer = hid.at[c, ring(y, -k if arriving else 0), :, :, halves[0]], plane_id(ring(y, k) * 4 + x)
        else:
            piece, peer = hid.at[c, :, ring(x, -k if arriving else 0), :, halves[1]], plane_id(y * 4 + ring(x, k))
        return push(piece, piece, d2_s.at[c, h * 3 + k - 1], d2_r.at[c, h * 3 + k - 1], peer)

    def d_relay(c):
        for h in (0, 1):
            for k in (1, 3, 2):
                d_first(c, h, k, True).wait_recv()
            for k in (2, 1, 3):
                d_second(c, h, k, False).start()

    def d_drain():
        for c in (0, 1):
            for h in (0, 1):
                for k in (1, 2, 3):
                    d_first(c, h, k, False).wait_send()
                    d_second(c, h, k, False).wait_send()

    drains.append(d_drain)

    diagonal = lax.broadcasted_iota(jnp.int32, (32, 128), 0) == lax.broadcasted_iota(jnp.int32, (32, 128), 1)

    def hidden(c):
        total = proj[c, me_t] + res[c * 16 : (c + 1) * 16].astype(F32)
        for k in range(1, 8):
            c_push(c, k).wait_recv()
            total = total + proj_recv[c, k].astype(F32)
        total = total.astype(BF16)
        hid[c, y, x] = total
        for k in (2, 1, 3):
            d_first(c, 0, k, False).start()
            d_first(c, 1, k, False).start()
        wide = total.astype(F32)
        squares = wide * wide
        partial = squares[:, 0:128]
        for j in range(1, 8):
            partial = partial + squares[:, j * 128 : (j + 1) * 128]
        return jnp.sum(partial, -1, keepdims=True)

    sums = [hidden(0), hidden(1)]
    d_relay(0)
    row = sum(jnp.sum(jnp.where(diagonal[16 * c : 16 * c + 16], sums[c], 0.0), 0, keepdims=True) for c in (0, 1))
    info[me_f, 8:16, :] = jnp.broadcast_to(row, (8, 128))

    def i_push(k):
        return push(info.at[me_f], info.at[me_f], i_s.at[k], i_r.at[k], feat_id(lax.rem(me_f + k, 16)))

    each(1, 16, lambda k: i_push(k).start())
    drains.append(lambda: each(1, 16, lambda k: i_push(k).wait_send()))
    d_relay(1)

    loaded(5)

    def target_tile(c, cols):
        term = jnp.dot(jnp.maximum(chosen[c].reshape(256, 1024), 0), wd[:, cols], preferred_element_type=F32)
        change[c, :, :, :, cols] = term.reshape(4, 4, 16, TILE)

    def ep_push(c, n):
        cols = slice(n * 512, (n + 1) * 512)
        return push(
            enc_send.at[c, :, 1 - core, :, cols], pair_recv.at[c, :, :, cols],
            ep_s.at[c, n], ep_r.at[c, n], feat_id(partner),
        )

    def encode(c):
        for h in (0, 1):
            for k in (1, 3, 2):
                d_second(c, h, k, True).wait_recv()

        def tile(cols):
            term = jnp.dot(hid[c].reshape(256, 1024), we[:, cols], preferred_element_type=F32)
            term = term.reshape(8, 2, 16, TILE)
            enc[c, :, :, :, cols] = term
            enc_send[c, :, :, :, cols] = term.astype(BF16)
            if cols.stop % 512 == 0:
                ep_push(c, cols.stop // 512 - 1).start()

        tiles(tile)
        drains.append(lambda: [ep_push(c, n).wait_send() for n in (0, 1)])

    SUMS = ((4, 2, 0), (-4, -2, 1), (3, 1, None), (-3, -1, None), (1, 1, None), (-1, -1, None), (2, 2, None), (-2, -2, None))

    def e_push(c, slot):
        _, target, half = SUMS[slot]
        cols = columns(half, 1024)
        return push(
            z_send.at[c, slot, :, cols], enc_recv.at[c, slot, :, cols], e_s.at[c, slot], e_r.at[c, slot],
            feat_id(chip(target) * 2 + core),
        )

    def e_part(c, slot):
        final, _, half = SUMS[slot]
        cols = columns(half, 1024)
        return enc[c, chip(final), core, :, cols] + pair_recv[c, chip(final), :, cols].astype(F32)

    def exchange(c):
        for n in (0, 1):
            ep_push(c, n).wait_recv()
        for slot in range(6):
            z_send[c, slot, :, columns(SUMS[slot][2], 1024)] = e_part(c, slot).astype(BF16)
            e_push(c, slot).start()

    def e_relay(c):
        for slot, near, half in ((6, 2, 0), (7, 3, 1)):
            e_push(c, near).wait_recv()
            e_push(c, half).wait_recv()
            total = e_part(c, slot) + enc_recv[c, near].astype(F32)
            cols, rest = columns(half, 1024), columns(1 - half, 1024)
            z_send[c, slot, :, cols] = (total[:, cols] + enc_recv[c, half, :, cols].astype(F32)).astype(BF16)
            z_send[c, slot, :, rest] = total[:, rest].astype(BF16)
            e_push(c, slot).start()
        drains.append(lambda: each(0, 8, lambda slot: e_push(c, slot).wait_send()))

    encode(0)
    exchange(0)

    encode(1)
    exchange(1)
    e_relay(0)

    each(1, 16, lambda k: i_push(k).wait_recv())
    total_info = info[0]
    for f in range(1, 16):
        total_info = total_info + info[f]
    scales[me_a] = jnp.sqrt(total_info[8:16] / D + EPSILON)
    bias_term = total_info[0:8]

    def s_push(k):
        return push(scales.at[me_a], scales.at[me_a], s_s.at[k], s_r.at[k], plane_id(lax.rem(me_a + k, 16)))

    each(1, 16, lambda k: s_push(k).start())
    drains.append(lambda: each(1, 16, lambda k: s_push(k).wait_send()))

    def as_column(a):
        row = jnp.broadcast_to(scales[a, 0:1], (32, 128))
        return jnp.sum(jnp.where(diagonal, row, 0.0), -1, keepdims=True)

    tiles(lambda cols: target_tile(0, cols))
    tiles(lambda cols: target_tile(1, cols))
    e_relay(1)

    each(1, 16, lambda k: s_push(k).wait_recv())
    loaded(12)
    inverse = 1.0 / as_column(me_f)
    lane = lax.broadcasted_iota(jnp.int32, (16, 128), 1)
    column = lax.broadcasted_iota(jnp.int32, (16, 1024), 1).astype(F32)

    def row_ids(c, f):
        return ids_col[pl.ds(pl.multiple_of(f * 32 + c * 16, 16), 16), :] - first_latent

    def u_push(c, k):
        piece = current.at[c, me_f]
        return push(piece, piece, u_s.at[c, k], u_r.at[c, k], feat_id(lax.rem(me_f + k, 16)))

    def latents(c):
        total = enc[c, z, core] + pair_recv[c, z].astype(F32)
        for k in (4, 5, 6, 7):
            e_push(c, k).wait_recv()
            total = total + enc_recv[c, k].astype(F32)
        scale = inverse[c * 16 : (c + 1) * 16]
        for j in range(8):
            cols = slice(j * 128, (j + 1) * 128)
            shift = be_ref[:, cols] - bias_term[j : j + 1]
            lat[c, z, core, :, cols] = jnp.maximum(total[:, cols] * scale + shift, 0.0).astype(BF16)
        mine = lat[c, z, core].astype(F32)
        ids = row_ids(c, me_f)
        held = jnp.zeros((16, 128), F32)
        for j in range(8):
            value = jnp.sum(jnp.where(ids[:, j : j + 1] == column, mine, 0.0), -1, keepdims=True)
            held = jnp.where(lane == j, value, held)
        current[c, me_f] = held.astype(BF16)
        for k in (8, 7, 9, 6, 10, 5, 11, 4, 12, 3, 13, 2, 14, 1, 15):
            u_push(c, k).start()
        drains.append(lambda: each(1, 16, lambda k: u_push(c, k).wait_send()))

    latents(0)
    latents(1)

    gathers = [
        gather_z(
            lat.at[c], lambda k, c=c: l_s.at[c, k], lambda k, c=c: l_r.at[c, k],
            lambda k, c=c: lp_s.at[c, k], lambda k, c=c: lp_r.at[c, k],
        )
        for c in (0, 1)
    ]
    for c in (0, 1):
        gathers[c][0]()

    def f_first(c, h, k):
        if h == 0:
            src, peer = chg_send.at[c, :, ring(x, k), :, halves[0]], plane_id(y * 4 + ring(x, k))
        else:
            src, peer = chg_send.at[c, ring(y, k), :, :, halves[1]], plane_id(ring(y, k) * 4 + x)
        return push(src, f1_in.at[c, h * 3 + k - 1], f1_s.at[c, h * 3 + k - 1], f1_r.at[c, h * 3 + k - 1], peer)

    def f_second(c, h, k):
        if h == 0:
            src, peer = part_send.at[c, 0, ring(y, k)], plane_id(ring(y, k) * 4 + x)
        else:
            src, peer = part_send.at[c, 1, ring(x, k)], plane_id(y * 4 + ring(x, k))
        return push(src, f2_in.at[c, h * 3 + k - 1], f2_s.at[c, h * 3 + k - 1], f2_r.at[c, h * 3 + k - 1], peer)

    def f_relay(c):
        for h in (0, 1):
            total = change[c, :, x, :, halves[0]] if h == 0 else change[c, y, :, :, halves[1]]
            for k in (1, 3, 2):
                f_first(c, h, k).wait_recv()
                total = total + f1_in[c, h * 3 + k - 1].astype(F32)
            part[c, h] = total
            part_send[c, h] = total.astype(BF16)
            for k in (2, 1, 3):
                f_second(c, h, k).start()

    def f_drain():
        for c in (0, 1):
            for h in (0, 1):
                for k in (1, 2, 3):
                    f_first(c, h, k).wait_send()
                    f_second(c, h, k).wait_send()

    def decode(c):
        each(1, 16, lambda k: u_push(c, k).wait_recv())

        def rebuild(f):
            slot = slots[c, f].astype(F32)
            values = current[c, f].astype(F32)
            best = jnp.zeros((16, 1024), F32)
            for j in range(8):
                best = jnp.where(slot == j + 1, values[:, j : j + 1], best)
            picked[f] = best.astype(BF16)

        each(0, 16, rebuild)

        def tile(cols):
            term = jnp.dot(picked[...].reshape(256, 1024), wd[:, cols], preferred_element_type=F32)
            term = change[c, :, :, :, cols] - term.reshape(4, 4, 16, TILE)
            change[c, :, :, :, cols] = term
            chg_send[c, :, :, :, cols] = term.astype(BF16)
            if cols.stop % 512 == 0:
                for k in (2, 1, 3):
                    f_first(c, cols.stop // 512 - 1, k).start()

        tiles(tile)

    decode(0)
    decode(1)
    for c in (0, 1):
        gathers[c][1]()
    f_relay(0)
    f_relay(1)
    drains.append(f_drain)

    for c in (0, 1):
        gathers[c][2]()

    own_scale = as_column(me_a)
    steered_out = [
        pltpu.make_async_copy(
            out_rows.at[c * 16 : (c + 1) * 16], steered_hbm.at[c * 16 : (c + 1) * 16], out_sem.at[2 + c]
        )
        for c in (0, 1)
    ]
    for c in (0, 1):
        rows = slice(c * 16, (c + 1) * 16)
        for h in (0, 1):
            total = part[c, h, y if h == 0 else x]
            for k in (1, 3, 2):
                f_second(c, h, k).wait_recv()
                total = total + f2_in[c, h * 3 + k - 1].astype(F32)
            own_hidden = hid[c, y, x, :, halves[h]].astype(F32)
            out_rows[rows, halves[h]] = (own_hidden + own_scale[rows] * total).astype(BF16)
        steered_out[c].start()

    latents_out = []
    for c in (0, 1):
        gathers[c][3]()
        rows = slice(c * 16, (c + 1) * 16)
        latents_out.append(pltpu.make_async_copy(lat.at[c], latents_hbm.at[:, :, rows], out_sem.at[c]))
        latents_out[c].start()

    for drain in drains:
        drain()
    for copy in latents_out + steered_out:
        copy.wait()


def hand_over(steered_in, latents_in, steered, latents, rows_a, rows_b, sem_in, sem_out):
    steps = [(steered_in, rows_a, steered)]
    for i in range(4):
        rows = pl.ds(i * 128, 128)
        steps.append((latents_in.at[rows], rows_b.at[rows], latents.at[rows]))
    arriving = [pltpu.make_async_copy(a, b, sem_in.at[i]) for i, (a, b, _) in enumerate(steps)]
    leaving = [pltpu.make_async_copy(b, c, sem_out.at[i]) for i, (_, b, c) in enumerate(steps)]
    for copy in arriving:
        copy.start()
    for into, out in zip(arriving, leaving):
        into.wait()
        out.start()
    for copy in leaving:
        copy.wait()


def local(
    new_queries, new_keys, new_values, key_cache, value_cache, cache_lengths, residual,
    output_weight, encoder_weight, encoder_bias, decoder_weight, decoder_bias, clamp_ids, clamp_values,
):
    hbm = pl.BlockSpec(memory_space=pl.ANY)
    V = pltpu.VMEM
    dma = pltpu.SemaphoreType.DMA
    steered, latents = pl.pallas_call(
        kernel,
        out_shape=(
            jax.ShapeDtypeStruct((32, 1024), BF16),
            jax.ShapeDtypeStruct((8, 2, 32, 1024), BF16),
        ),
        in_specs=[hbm] * 14,
        out_specs=(hbm, hbm),
        scratch_shapes=[
            V((16, 2048), BF16), V((16, 256, 128), BF16), V((16, 256, 128), BF16), V((32, 1024), BF16),
            V((2048, 1024), BF16), V((1024, 1024), BF16), V((1024, 1024), BF16),
            V((16, 128), BF16), V((16, 128), BF16), pltpu.SMEM((16,), jnp.int32), V((1, 1024), F32), V((1, 1024), F32),
            V((8, 512), jnp.int32), V((8, 512), jnp.int32),
            V((16, 16, 128), F32), V((16, 16, 128), F32),
            V((16, 16, 128), F32), V((16, 16, 128), F32), V((16, 16, 256), F32), V((16, 16, 256), BF16),
            V((512, 8), F32), V((512, 8), F32), V((2, 16, 16, 1024), BF16), V((2, 16, 16, 1024), BF16),
            V((2, 4, 4, 16, 1024), F32),
            V((16, 16, 1024), BF16), V((2, 16, 16, 128), BF16),
            V((8, 2, 16, 2048), BF16), V((2, 8, 16, 1024), F32), V((2, 8, 16, 1024), BF16), V((2, 8, 16, 1024), BF16),
            V((2, 4, 4, 16, 1024), BF16), V((16, 16, 128), F32), V((16, 8, 128), F32),
            V((2, 8, 2, 16, 1024), F32), V((2, 8, 2, 16, 1024), BF16), V((2, 8, 16, 1024), BF16),
            V((2, 8, 16, 1024), BF16), V((2, 8, 16, 1024), BF16), V((2, 8, 2, 16, 1024), BF16),
            V((2, 4, 4, 16, 1024), BF16), V((2, 6, 4, 16, 512), BF16), V((2, 2, 4, 16, 512), F32),
            V((2, 2, 4, 16, 512), BF16), V((2, 6, 16, 512), BF16), V((32, 1024), BF16),
            dma((14,)), dma((4,)),
            dma((8,)), dma((8,)), dma((9,)), dma((9,)), dma((2, 8)), dma((2, 8)),
            dma((2, 6)), dma((2, 6)), dma((2, 6)), dma((2, 6)), dma((16,)), dma((16,)), dma((16,)), dma((16,)),
            dma((2, 2)), dma((2, 2)), dma((2, 8)), dma((2, 8)), dma((2, 16)), dma((2, 16)),
            dma((2, 8)), dma((2, 8)), dma((2, 9)), dma((2, 9)),
            dma((2, 6)), dma((2, 6)), dma((2, 6)), dma((2, 6)),
        ],
        compiler_params=pltpu.CompilerParams(
            collective_id=0, has_side_effects=True, vmem_limit_bytes=62 * 2**20
        ),
    )(
        new_queries, new_keys, new_values, key_cache, value_cache, cache_lengths, residual,
        output_weight, encoder_weight, encoder_bias.reshape(1, 1024), decoder_weight,
        decoder_bias.reshape(1, 1024), clamp_ids.T, clamp_values.T,
    )
    return pl.pallas_call(
        hand_over,
        out_shape=(jax.ShapeDtypeStruct((32, 1024), BF16), jax.ShapeDtypeStruct((512, 1024), BF16)),
        in_specs=[hbm, hbm],
        out_specs=(hbm, hbm),
        scratch_shapes=[V((32, 1024), BF16), V((512, 1024), BF16), dma((5,)), dma((5,))],
        compiler_params=pltpu.CompilerParams(vmem_limit_bytes=62 * 2**20),
    )(steered, latents.reshape(512, 1024))


def solution(mesh):
    in_specs = (
        P(("section", "feat"), "tensor"),
        P(("section", "feat"), "tensor"),
        P(("section", "feat"), "tensor"),
        P(("section", "feat"), None, "tensor"),
        P(("section", "feat"), None, "tensor"),
        P(("section", "feat")),
        P("section", "feat"),
        P("tensor", "feat"),
        P("feat", ("section", "tensor")),
        P(("section", "tensor")),
        P(("section", "tensor"), "feat"),
        P("feat"),
        P(),
        P(),
    )
    out_specs = (P(("section", "tensor"), "feat"), P(None, ("section", "tensor")))
    return jax.shard_map(local, mesh=mesh, in_specs=in_specs, out_specs=out_specs, check_vma=False)
```

```python
import functools
import math

import jax
import jax.numpy as jnp
from jax import lax
from jax.experimental import pallas as pl
from jax.experimental.pallas import tpu as pltpu
from jax.sharding import PartitionSpec as P

D = 16384
HD = 128
EPSILON = 1e-05
NEGATIVE = -1e30
MESH = pl.DeviceIdType.MESH
F32 = jnp.float32
BF16 = jnp.bfloat16

TILE = 256


def kernel(
    q_hbm, nk_hbm, nv_hbm, kc_hbm, vc_hbm, lens_hbm, res_hbm, wo_hbm, we_hbm,
    be_hbm, wd_hbm, bd_hbm, ids_hbm, vals_hbm,
    steered_hbm, latents_hbm,
    q_in, kc, vc, res, wo, we, wd, nk_ref, nv_ref, lens_ref, be_ref, bd_ref, ids_ref, vals_ref, q_heads, o_heads,
    keys_wide, values_wide, scores_all, weights,
    ids_col, vals_col, chosen, slots, change, picked, current,
    att, proj, proj_send, proj_recv, hid, info, scales,
    enc, enc_send, pair_recv, z_send, enc_recv, lat, chg_send, f1_in, part, part_send, f2_in, out_rows,
    in_sem, out_sem,
    b_s, b_r, bp_s, bp_r, c_s, c_r, d1_s, d1_r, d2_s, d2_r, i_s, i_r, s_s, s_r,
    ep_s, ep_r, e_s, e_r, u_s, u_r, l_s, l_r, lp_s, lp_r, f1_s, f1_r, f2_s, f2_r,
):
    me_f = lax.axis_index("feat")
    me_t = lax.axis_index("tensor")
    me_a = lax.axis_index("section") * 8 + me_t
    z = me_f // 2
    core = lax.rem(me_f, 2)
    partner = me_f + 1 - 2 * core
    y, x = me_a // 4, lax.rem(me_a, 4)
    halves = (slice(0, 512), slice(512, 1024))

    def feat_id(f):
        return {"feat": f}

    def plane_id(a):
        return {"section": a // 8, "tensor": lax.rem(a, 8)}

    def each(first, last, do):
        for k in range(first, last):
            do(k)

    def push(src, dst, ss, rs, device):
        return pltpu.make_async_remote_copy(
            src_ref=src, dst_ref=dst, send_sem=ss, recv_sem=rs,
            device_id=device, device_id_type=MESH,
        )

    loads = [
        pltpu.make_async_copy(q_hbm, q_in, in_sem.at[0]),
        pltpu.make_async_copy(kc_hbm, kc, in_sem.at[1]),
        pltpu.make_async_copy(vc_hbm, vc, in_sem.at[2]),
        pltpu.make_async_copy(wo_hbm, wo, in_sem.at[3]),
        pltpu.make_async_copy(we_hbm, we, in_sem.at[4]),
        pltpu.make_async_copy(wd_hbm, wd, in_sem.at[5]),
        pltpu.make_async_copy(res_hbm.at[pl.ds(me_t * 32, 32)], res, in_sem.at[6]),
        pltpu.make_async_copy(nk_hbm, nk_ref, in_sem.at[7]),
        pltpu.make_async_copy(nv_hbm, nv_ref, in_sem.at[8]),
        pltpu.make_async_copy(lens_hbm, lens_ref, in_sem.at[9]),
        pltpu.make_async_copy(ids_hbm, ids_ref, in_sem.at[10]),
        pltpu.make_async_copy(vals_hbm, vals_ref, in_sem.at[11]),
        pltpu.make_async_copy(be_hbm, be_ref, in_sem.at[12]),
        pltpu.make_async_copy(bd_hbm, bd_ref, in_sem.at[13]),
    ]
    for i in (0, 1, 2, 7, 8, 9, 10, 11):
        loads[i].start()

    barrier = pltpu.get_barrier_semaphore()

    def announce(k):
        pl.semaphore_signal(barrier, inc=1, device_id=feat_id(lax.rem(me_f + k, 16)), device_id_type=MESH)
        pl.semaphore_signal(barrier, inc=1, device_id=plane_id(lax.rem(me_a + k, 16)), device_id_type=MESH)

    each(1, 16, announce)

    waited = set()

    def loaded(i):
        if i not in waited:
            waited.add(i)
            loads[i].wait()

    drains = []

    loaded(0)
    for h in range(16):
        q_heads[:, h, :] = q_in[:, h * HD : (h + 1) * HD].astype(F32)
    loaded(7)
    loaded(8)
    loaded(9)
    fresh_keys = nk_ref[...].astype(F32)
    fresh_values = nv_ref[...].astype(F32)
    loaded(1)
    loaded(2)
    for i in (3, 6, 12, 13, 4, 5):
        loads[i].start()
    score_scale = 1.0 / math.sqrt(HD)
    position = lax.broadcasted_iota(jnp.int32, (16, 256), 1)
    for r in range(16):
        keys_wide[r] = jnp.broadcast_to(fresh_keys[r : r + 1], (16, 128))
        values_wide[r] = jnp.broadcast_to(fresh_values[r : r + 1], (16, 128))
    for r in range(16):
        scores = lax.dot_general(
            q_heads[r].astype(BF16), kc[r], (((1,), (1,)), ((), ())), preferred_element_type=F32
        ) * score_scale
        scores_all[r] = jnp.where(position < lens_ref[r], scores, NEGATIVE)
    scores = scores_all[...]
    own_score = jnp.sum(q_heads[...] * keys_wide[...], -1, keepdims=True) * score_scale
    highest = jnp.maximum(jnp.max(scores, -1, keepdims=True), own_score)
    raw = jnp.exp(scores - highest)
    own_raw = jnp.exp(own_score - highest)
    totals = jnp.sum(raw, -1, keepdims=True) + own_raw
    weights[...] = raw.astype(BF16)
    for r in range(16):
        o_heads[r] = jnp.dot(weights[r], vc[r], preferred_element_type=F32)
    own_part = own_raw.astype(BF16).astype(F32) * values_wide[...]
    o_heads[...] = (o_heads[...] + own_part) * (1.0 / totals)
    for h in range(16):
        att[z, core, :, h * HD : (h + 1) * HD] = o_heads[:, h, :].astype(BF16)

    pl.semaphore_wait(barrier, 30)

    GATHER = ((0, 2, None), (0, -2, None), (0, 1, None), (0, -1, None), (-2, 1, None), (2, -1, None), (-2, 2, 0), (2, -2, 1))

    def chip(step):
        return lax.rem(z + step + 8, 8)

    def columns(half, width):
        return slice(0, width) if half is None else slice(half * width // 2, (half + 1) * width // 2)

    def gather_z(buf, send, recv, across_send, across_recv):
        width = buf.shape[-1]

        def hop(slot, arriving):
            block, target, half = GATHER[slot]
            piece = buf.at[chip(block - target if arriving else block), core, :, columns(half, width)]
            return push(piece, piece, send(slot), recv(slot), feat_id(chip(target) * 2 + core))

        def across(slot, arriving):
            block, half = (0, None) if slot == 8 else (GATHER[slot][0] - GATHER[slot][1], GATHER[slot][2])
            piece = buf.at[chip(block), 1 - core if arriving else core, :, columns(half, width)]
            return push(piece, piece, across_send(slot), across_recv(slot), feat_id(partner))

        def start():
            for slot in range(4):
                hop(slot, False).start()
            across(8, False).start()

        def relay():
            for slot, follow in ((0, (6, 4)), (1, (7, 5))):
                hop(slot, True).wait_recv()
                for k in follow:
                    hop(k, False).start()

        def spread():
            for slot in (0, 1):
                across(slot, False).start()
            for slot in range(2, 8):
                hop(slot, True).wait_recv()
                across(slot, False).start()

        def finish():
            for slot in range(9):
                across(slot, True).wait_recv()

        def drain():
            for slot in range(8):
                hop(slot, False).wait_send()
            for slot in range(9):
                across(slot, False).wait_send()

        drains.append(drain)
        return start, relay, spread, finish

    b_start, b_relay, b_spread, b_finish = gather_z(
        att, lambda k: b_s.at[k], lambda k: b_r.at[k], lambda k: bp_s.at[k], lambda k: bp_r.at[k]
    )
    b_start()

    loaded(10)
    loaded(11)
    ids_col[...] = ids_ref[...].astype(F32).T
    vals_col[...] = vals_ref[...].astype(F32).T
    first_latent = (me_a * 1024).astype(F32)

    def choose(i, carry):
        rows = pl.ds(pl.multiple_of(i * 32, 32), 32)
        ids = ids_col[rows, :] - first_latent
        values = vals_col[rows, :]
        column = lax.broadcasted_iota(jnp.int32, (32, 1024), 1).astype(F32)
        best = jnp.full((32, 1024), -1.0, F32)
        slot = jnp.zeros((32, 1024), F32)
        for j in range(8):
            same = ids[:, j : j + 1] == column
            best = jnp.where(same, jnp.maximum(best, values[:, j : j + 1]), best)
            slot = jnp.where(same, j + 1.0, slot)
        chosen[0, i] = best[0:16].astype(BF16)
        chosen[1, i] = best[16:32].astype(BF16)
        slots[0, i] = slot[0:16].astype(BF16)
        slots[1, i] = slot[16:32].astype(BF16)
        return carry

    lax.fori_loop(0, 8, choose, 0)
    b_relay()
    lax.fori_loop(8, 16, choose, 0)
    b_spread()
    loaded(3)
    b_finish()

    def tiles(do):
        for n in range(1024 // TILE):
            do(slice(n * TILE, (n + 1) * TILE))

    def c_push(c, k):
        peer = lax.rem(me_t + k, 8)
        return push(proj_send.at[c, peer], proj_recv.at[c, k], c_s.at[c, k], c_r.at[c, k], {"tensor": peer})

    def project(c):
        def tile(cols):
            term = jnp.dot(att[:, c].reshape(128, 2048), wo[:, cols], preferred_element_type=F32).reshape(8, 16, TILE)
            proj[c, :, :, cols] = term
            proj_send[c, :, :, cols] = term.astype(BF16)

        tiles(tile)
        each(1, 8, lambda k: c_push(c, k).start())
        drains.append(lambda: each(1, 8, lambda k: c_push(c, k).wait_send()))

    project(0)
    project(1)

    loaded(4)
    loaded(13)
    bias = bd_ref[...]
    high = bias.astype(BF16)
    rest = bias - high.astype(F32)
    middle = rest.astype(BF16)
    low = (rest - middle.astype(F32)).astype(BF16)
    index = lax.broadcasted_iota(jnp.int32, (16, 1024), 0)
    stacked = jnp.where(
        index == 0, high.astype(F32), jnp.where(index == 1, middle.astype(F32), jnp.where(index == 2, low.astype(F32), 0.0))
    ).astype(BF16)
    for n in range(4):
        term = jnp.dot(stacked, we[:, n * 256 : (n + 1) * 256], preferred_element_type=F32)
        term = jnp.sum(term[0:8], 0, keepdims=True)
        info[me_f, 2 * n : 2 * n + 1, :] = term[:, :128]
        info[me_f, 2 * n + 1 : 2 * n + 2, :] = term[:, 128:]

    loaded(6)

    def ring(place, step):
        return lax.rem(place + step + 4, 4)

    def d_first(c, h, k, arriving):
        yy, xx = (y, ring(x, -k if arriving else 0)) if h == 0 else (ring(y, -k if arriving else 0), x)
        peer = plane_id(y * 4 + ring(x, k)) if h == 0 else plane_id(ring(y, k) * 4 + x)
        piece = hid.at[c, yy, xx, :, halves[h]]
        return push(piece, piece, d1_s.at[c, h * 3 + k - 1], d1_r.at[c, h * 3 + k - 1], peer)

    def d_second(c, h, k, arriving):
        if h == 0:
            piece, peer = hid.at[c, ring(y, -k if arriving else 0), :, :, halves[0]], plane_id(ring(y, k) * 4 + x)
        else:
            piece, peer = hid.at[c, :, ring(x, -k if arriving else 0), :, halves[1]], plane_id(y * 4 + ring(x, k))
        return push(piece, piece, d2_s.at[c, h * 3 + k - 1], d2_r.at[c, h * 3 + k - 1], peer)

    def d_relay(c):
        for h in (0, 1):
            for k in (1, 3, 2):
                d_first(c, h, k, True).wait_recv()
            for k in (2, 1, 3):
                d_second(c, h, k, False).start()

    def d_drain():
        for c in (0, 1):
            for h in (0, 1):
                for k in (1, 2, 3):
                    d_first(c, h, k, False).wait_send()
                    d_second(c, h, k, False).wait_send()

    drains.append(d_drain)

    diagonal = lax.broadcasted_iota(jnp.int32, (32, 128), 0) == lax.broadcasted_iota(jnp.int32, (32, 128), 1)

    def hidden(c):
        total = proj[c, me_t] + res[c * 16 : (c + 1) * 16].astype(F32)
        for k in range(1, 8):
            c_push(c, k).wait_recv()
            total = total + proj_recv[c, k].astype(F32)
        total = total.astype(BF16)
        hid[c, y, x] = total
        for k in (2, 1, 3):
            d_first(c, 0, k, False).start()
            d_first(c, 1, k, False).start()
        wide = total.astype(F32)
        squares = wide * wide
        partial = squares[:, 0:128]
        for j in range(1, 8):
            partial = partial + squares[:, j * 128 : (j + 1) * 128]
        return jnp.sum(partial, -1, keepdims=True)

    sums = [hidden(0), hidden(1)]
    d_relay(0)
    row = sum(jnp.sum(jnp.where(diagonal[16 * c : 16 * c + 16], sums[c], 0.0), 0, keepdims=True) for c in (0, 1))
    info[me_f, 8:16, :] = jnp.broadcast_to(row, (8, 128))

    def i_push(k):
        return push(info.at[me_f], info.at[me_f], i_s.at[k], i_r.at[k], feat_id(lax.rem(me_f + k, 16)))

    each(1, 16, lambda k: i_push(k).start())
    drains.append(lambda: each(1, 16, lambda k: i_push(k).wait_send()))
    d_relay(1)

    loaded(5)

    def target_tile(c, cols):
        term = jnp.dot(jnp.maximum(chosen[c].reshape(256, 1024), 0), wd[:, cols], preferred_element_type=F32)
        change[c, :, :, :, cols] = term.reshape(4, 4, 16, TILE)

    def ep_push(c, n):
        cols = slice(n * 512, (n + 1) * 512)
        return push(
            enc_send.at[c, :, 1 - core, :, cols], pair_recv.at[c, :, :, cols],
            ep_s.at[c, n], ep_r.at[c, n], feat_id(partner),
        )

    def encode(c):
        for h in (0, 1):
            for k in (1, 3, 2):
                d_second(c, h, k, True).wait_recv()

        def tile(cols):
            term = jnp.dot(hid[c].reshape(256, 1024), we[:, cols], preferred_element_type=F32)
            term = term.reshape(8, 2, 16, TILE)
            enc[c, :, :, :, cols] = term
            enc_send[c, :, :, :, cols] = term.astype(BF16)
            if cols.stop % 512 == 0:
                ep_push(c, cols.stop // 512 - 1).start()

        tiles(tile)
        drains.append(lambda: [ep_push(c, n).wait_send() for n in (0, 1)])

    SUMS = ((4, 2, 0), (-4, -2, 1), (3, 1, None), (-3, -1, None), (1, 1, None), (-1, -1, None), (2, 2, None), (-2, -2, None))

    def e_push(c, slot):
        _, target, half = SUMS[slot]
        cols = columns(half, 1024)
        return push(
            z_send.at[c, slot, :, cols], enc_recv.at[c, slot, :, cols], e_s.at[c, slot], e_r.at[c, slot],
            feat_id(chip(target) * 2 + core),
        )

    def e_part(c, slot):
        final, _, half = SUMS[slot]
        cols = columns(half, 1024)
        return enc[c, chip(final), core, :, cols] + pair_recv[c, chip(final), :, cols].astype(F32)

    def exchange(c):
        for n in (0, 1):
            ep_push(c, n).wait_recv()
        for slot in range(6):
            z_send[c, slot, :, columns(SUMS[slot][2], 1024)] = e_part(c, slot).astype(BF16)
            e_push(c, slot).start()

    def e_relay(c):
        for slot, near, half in ((6, 2, 0), (7, 3, 1)):
            e_push(c, near).wait_recv()
            e_push(c, half).wait_recv()
            total = e_part(c, slot) + enc_recv[c, near].astype(F32)
            cols, rest = columns(half, 1024), columns(1 - half, 1024)
            z_send[c, slot, :, cols] = (total[:, cols] + enc_recv[c, half, :, cols].astype(F32)).astype(BF16)
            z_send[c, slot, :, rest] = total[:, rest].astype(BF16)
            e_push(c, slot).start()
        drains.append(lambda: each(0, 8, lambda slot: e_push(c, slot).wait_send()))

    encode(0)
    exchange(0)

    encode(1)
    exchange(1)
    e_relay(0)

    each(1, 16, lambda k: i_push(k).wait_recv())
    total_info = info[0]
    for f in range(1, 16):
        total_info = total_info + info[f]
    scales[me_a] = jnp.sqrt(total_info[8:16] / D + EPSILON)
    bias_term = total_info[0:8]

    def s_push(k):
        return push(scales.at[me_a], scales.at[me_a], s_s.at[k], s_r.at[k], plane_id(lax.rem(me_a + k, 16)))

    each(1, 16, lambda k: s_push(k).start())
    drains.append(lambda: each(1, 16, lambda k: s_push(k).wait_send()))

    def as_column(a):
        row = jnp.broadcast_to(scales[a, 0:1], (32, 128))
        return jnp.sum(jnp.where(diagonal, row, 0.0), -1, keepdims=True)

    tiles(lambda cols: target_tile(0, cols))
    tiles(lambda cols: target_tile(1, cols))
    e_relay(1)

    each(1, 16, lambda k: s_push(k).wait_recv())
    loaded(12)
    inverse = 1.0 / as_column(me_f)
    lane = lax.broadcasted_iota(jnp.int32, (16, 128), 1)
    column = lax.broadcasted_iota(jnp.int32, (16, 1024), 1).astype(F32)

    def row_ids(c, f):
        return ids_col[pl.ds(pl.multiple_of(f * 32 + c * 16, 16), 16), :] - first_latent

    def u_push(c, k):
        piece = current.at[c, me_f]
        return push(piece, piece, u_s.at[c, k], u_r.at[c, k], feat_id(lax.rem(me_f + k, 16)))

    def latents(c):
        total = enc[c, z, core] + pair_recv[c, z].astype(F32)
        for k in (4, 5, 6, 7):
            e_push(c, k).wait_recv()
            total = total + enc_recv[c, k].astype(F32)
        scale = inverse[c * 16 : (c + 1) * 16]
        for j in range(8):
            cols = slice(j * 128, (j + 1) * 128)
            shift = be_ref[:, cols] - bias_term[j : j + 1]
            lat[c, z, core, :, cols] = jnp.maximum(total[:, cols] * scale + shift, 0.0).astype(BF16)
        mine = lat[c, z, core].astype(F32)
        ids = row_ids(c, me_f)
        held = jnp.zeros((16, 128), F32)
        for j in range(8):
            value = jnp.sum(jnp.where(ids[:, j : j + 1] == column, mine, 0.0), -1, keepdims=True)
            held = jnp.where(lane == j, value, held)
        current[c, me_f] = held.astype(BF16)
        for k in (8, 7, 9, 6, 10, 5, 11, 4, 12, 3, 13, 2, 14, 1, 15):
            u_push(c, k).start()
        drains.append(lambda: each(1, 16, lambda k: u_push(c, k).wait_send()))

    gathers = [
        gather_z(
            lat.at[c], lambda k, c=c: l_s.at[c, k], lambda k, c=c: l_r.at[c, k],
            lambda k, c=c: lp_s.at[c, k], lambda k, c=c: lp_r.at[c, k],
        )
        for c in (0, 1)
    ]
    latents(0)
    gathers[0][0]()
    latents(1)
    gathers[1][0]()

    def f_first(c, h, k):
        if h == 0:
            src, peer = chg_send.at[c, :, ring(x, k), :, halves[0]], plane_id(y * 4 + ring(x, k))
        else:
            src, peer = chg_send.at[c, ring(y, k), :, :, halves[1]], plane_id(ring(y, k) * 4 + x)
        return push(src, f1_in.at[c, h * 3 + k - 1], f1_s.at[c, h * 3 + k - 1], f1_r.at[c, h * 3 + k - 1], peer)

    def f_second(c, h, k):
        if h == 0:
            src, peer = part_send.at[c, 0, ring(y, k)], plane_id(ring(y, k) * 4 + x)
        else:
            src, peer = part_send.at[c, 1, ring(x, k)], plane_id(y * 4 + ring(x, k))
        return push(src, f2_in.at[c, h * 3 + k - 1], f2_s.at[c, h * 3 + k - 1], f2_r.at[c, h * 3 + k - 1], peer)

    def f_relay(c):
        for h in (0, 1):
            total = change[c, :, x, :, halves[0]] if h == 0 else change[c, y, :, :, halves[1]]
            for k in (1, 3, 2):
                f_first(c, h, k).wait_recv()
                total = total + f1_in[c, h * 3 + k - 1].astype(F32)
            part[c, h] = total
            part_send[c, h] = total.astype(BF16)
            for k in (2, 1, 3):
                f_second(c, h, k).start()

    def f_drain():
        for c in (0, 1):
            for h in (0, 1):
                for k in (1, 2, 3):
                    f_first(c, h, k).wait_send()
                    f_second(c, h, k).wait_send()

    def decode(c):
        each(1, 16, lambda k: u_push(c, k).wait_recv())

        def rebuild(f):
            slot = slots[c, f].astype(F32)
            values = current[c, f].astype(F32)
            best = jnp.zeros((16, 1024), F32)
            for j in range(8):
                best = jnp.where(slot == j + 1, values[:, j : j + 1], best)
            picked[f] = best.astype(BF16)

        each(0, 16, rebuild)

        def tile(cols):
            term = jnp.dot(picked[...].reshape(256, 1024), wd[:, cols], preferred_element_type=F32)
            term = change[c, :, :, :, cols] - term.reshape(4, 4, 16, TILE)
            change[c, :, :, :, cols] = term
            chg_send[c, :, :, :, cols] = term.astype(BF16)
            if cols.stop % 512 == 0:
                for k in (2, 1, 3):
                    f_first(c, cols.stop // 512 - 1, k).start()

        tiles(tile)

    decode(0)
    decode(1)
    for c in (0, 1):
        gathers[c][1]()
    f_relay(0)
    f_relay(1)
    drains.append(f_drain)

    for c in (0, 1):
        gathers[c][2]()

    own_scale = as_column(me_a)
    steered_out = [
        pltpu.make_async_copy(
            out_rows.at[c * 16 : (c + 1) * 16], steered_hbm.at[c * 16 : (c + 1) * 16], out_sem.at[2 + c]
        )
        for c in (0, 1)
    ]
    for c in (0, 1):
        rows = slice(c * 16, (c + 1) * 16)
        for h in (0, 1):
            total = part[c, h, y if h == 0 else x]
            for k in (1, 3, 2):
                f_second(c, h, k).wait_recv()
                total = total + f2_in[c, h * 3 + k - 1].astype(F32)
            own_hidden = hid[c, y, x, :, halves[h]].astype(F32)
            out_rows[rows, halves[h]] = (own_hidden + own_scale[rows] * total).astype(BF16)
        steered_out[c].start()

    latents_out = []
    for c in (0, 1):
        gathers[c][3]()
        rows = slice(c * 16, (c + 1) * 16)
        latents_out.append(pltpu.make_async_copy(lat.at[c], latents_hbm.at[:, :, rows], out_sem.at[c]))
        latents_out[c].start()

    for drain in drains:
        drain()
    for copy in latents_out + steered_out:
        copy.wait()


def hand_over(steered_in, latents_in, steered, latents, rows_a, rows_b, sem_in, sem_out):
    steps = [(steered_in, rows_a, steered)]
    for i in range(4):
        rows = pl.ds(i * 128, 128)
        steps.append((latents_in.at[rows], rows_b.at[rows], latents.at[rows]))
    arriving = [pltpu.make_async_copy(a, b, sem_in.at[i]) for i, (a, b, _) in enumerate(steps)]
    leaving = [pltpu.make_async_copy(b, c, sem_out.at[i]) for i, (_, b, c) in enumerate(steps)]
    for copy in arriving:
        copy.start()
    for into, out in zip(arriving, leaving):
        into.wait()
        out.start()
    for copy in leaving:
        copy.wait()


def local(
    new_queries, new_keys, new_values, key_cache, value_cache, cache_lengths, residual,
    output_weight, encoder_weight, encoder_bias, decoder_weight, decoder_bias, clamp_ids, clamp_values,
):
    hbm = pl.BlockSpec(memory_space=pl.ANY)
    V = pltpu.VMEM
    dma = pltpu.SemaphoreType.DMA
    steered, latents = pl.pallas_call(
        kernel,
        out_shape=(
            jax.ShapeDtypeStruct((32, 1024), BF16),
            jax.ShapeDtypeStruct((8, 2, 32, 1024), BF16),
        ),
        in_specs=[hbm] * 14,
        out_specs=(hbm, hbm),
        scratch_shapes=[
            V((16, 2048), BF16), V((16, 256, 128), BF16), V((16, 256, 128), BF16), V((32, 1024), BF16),
            V((2048, 1024), BF16), V((1024, 1024), BF16), V((1024, 1024), BF16),
            V((16, 128), BF16), V((16, 128), BF16), pltpu.SMEM((16,), jnp.int32), V((1, 1024), F32), V((1, 1024), F32),
            V((8, 512), jnp.int32), V((8, 512), jnp.int32),
            V((16, 16, 128), F32), V((16, 16, 128), F32),
            V((16, 16, 128), F32), V((16, 16, 128), F32), V((16, 16, 256), F32), V((16, 16, 256), BF16),
            V((512, 8), F32), V((512, 8), F32), V((2, 16, 16, 1024), BF16), V((2, 16, 16, 1024), BF16),
            V((2, 4, 4, 16, 1024), F32),
            V((16, 16, 1024), BF16), V((2, 16, 16, 128), BF16),
            V((8, 2, 16, 2048), BF16), V((2, 8, 16, 1024), F32), V((2, 8, 16, 1024), BF16), V((2, 8, 16, 1024), BF16),
            V((2, 4, 4, 16, 1024), BF16), V((16, 16, 128), F32), V((16, 8, 128), F32),
            V((2, 8, 2, 16, 1024), F32), V((2, 8, 2, 16, 1024), BF16), V((2, 8, 16, 1024), BF16),
            V((2, 8, 16, 1024), BF16), V((2, 8, 16, 1024), BF16), V((2, 8, 2, 16, 1024), BF16),
            V((2, 4, 4, 16, 1024), BF16), V((2, 6, 4, 16, 512), BF16), V((2, 2, 4, 16, 512), F32),
            V((2, 2, 4, 16, 512), BF16), V((2, 6, 16, 512), BF16), V((32, 1024), BF16),
            dma((14,)), dma((4,)),
            dma((8,)), dma((8,)), dma((9,)), dma((9,)), dma((2, 8)), dma((2, 8)),
            dma((2, 6)), dma((2, 6)), dma((2, 6)), dma((2, 6)), dma((16,)), dma((16,)), dma((16,)), dma((16,)),
            dma((2, 2)), dma((2, 2)), dma((2, 8)), dma((2, 8)), dma((2, 16)), dma((2, 16)),
            dma((2, 8)), dma((2, 8)), dma((2, 9)), dma((2, 9)),
            dma((2, 6)), dma((2, 6)), dma((2, 6)), dma((2, 6)),
        ],
        compiler_params=pltpu.CompilerParams(
            collective_id=0, has_side_effects=True, vmem_limit_bytes=62 * 2**20
        ),
    )(
        new_queries, new_keys, new_values, key_cache, value_cache, cache_lengths, residual,
        output_weight, encoder_weight, encoder_bias.reshape(1, 1024), decoder_weight,
        decoder_bias.reshape(1, 1024), clamp_ids.T, clamp_values.T,
    )
    return pl.pallas_call(
        hand_over,
        out_shape=(jax.ShapeDtypeStruct((32, 1024), BF16), jax.ShapeDtypeStruct((512, 1024), BF16)),
        in_specs=[hbm, hbm],
        out_specs=(hbm, hbm),
        scratch_shapes=[V((32, 1024), BF16), V((512, 1024), BF16), dma((5,)), dma((5,))],
        compiler_params=pltpu.CompilerParams(vmem_limit_bytes=62 * 2**20),
    )(steered, latents.reshape(512, 1024))


def solution(mesh):
    in_specs = (
        P(("section", "feat"), "tensor"),
        P(("section", "feat"), "tensor"),
        P(("section", "feat"), "tensor"),
        P(("section", "feat"), None, "tensor"),
        P(("section", "feat"), None, "tensor"),
        P(("section", "feat")),
        P("section", "feat"),
        P("tensor", "feat"),
        P("feat", ("section", "tensor")),
        P(("section", "tensor")),
        P(("section", "tensor"), "feat"),
        P("feat"),
        P(),
        P(),
    )
    out_specs = (P(("section", "tensor"), "feat"), P(None, ("section", "tensor")))
    return jax.shard_map(local, mesh=mesh, in_specs=in_specs, out_specs=out_specs, check_vma=False)
```
